32 devices in a mesh: slab: 4 (over y, x), chan: 8 (over z, core).
Axes of the slice: x: 2, y: 2, z: 4, core: 2. Of those that a mesh axis runs over, the one named last changes fastest.
Arguments:
- volume: bfloat16 [8, 16, 64, 256], P('slab', 'chan'), may hold values from -6 to 6
- weights: bfloat16 [6912, 256], P(None, 'slab'), may hold values from -0.078125 to 0.078125
Outputs:
- conv_out: bfloat16 [8, 16, 64, 256], P('slab', 'chan')
The draws below stay inside these ranges and needn't reach their ends.
All inputs are finite; a program needn't handle non-finite values.
Results may differ from the reference program's by a relative error of at most 0.001.
Values may be sent and summed in bfloat16 or wider, within the bound.
No kernel may reach another device: no remote copies, remote signals or barrier semaphores. Data moves between devices by JAX's collectives and lax.ppermute only.
A program may use at most 64 MiB of HBM per device.

```python
import jax
import jax.numpy as jnp
from jax import lax

C = 256
COLS = 64
DEPTH = 8
ROWS = 16


def block_scale(own_key, shape, split, least, largest):
    gain = 1.0
    for position, blocks in split:
        draws = jax.random.uniform(jax.random.fold_in(jax.random.fold_in(own_key, 6), position), (blocks,), jnp.float32, least / len(split), largest / len(split))
        gain = gain * jnp.repeat(jnp.exp(draws), shape[position] // blocks).reshape((-1,) + (1,) * (len(shape) - 1 - position))
    return gain


def scatter_about(stream_key, extent, width, limit, shards=(), kind=jnp.bfloat16):
    array = jax.random.normal(stream_key, extent, jnp.float32) * width
    if len(shards) > 0:
        array = block_scale(stream_key, extent, shards, -0.22, 0.18) * array
    return jnp.clip(array, min=-limit, max=limit).astype(kind)


def setup_inputs(seed: int = 0) -> dict:
    key_list = jax.random.split(jax.random.key(seed), 3)
    return {
        "volume": scatter_about(key_list[0], (DEPTH, ROWS, COLS, C), 1.0, 6.0, ((0, 4), (1, 8))),
        "weights": scatter_about(key_list[1], (27 * C, C), (27 * C) ** -0.5, 0.078125, ((1, 4),)),
    }


def reference(volume, weights):
    padded = jnp.pad(volume, ((1, 1), (1, 1), (1, 1), (0, 0)))
    kernel = weights.reshape(27, C, C)

    def one_plane(depth_index):
        three_planes = lax.dynamic_slice_in_dim(padded, depth_index, 3, 0)
        summed = jnp.zeros((ROWS * COLS, C), jnp.float32)
        for depth_off in range(3):
            for row_off in range(3):
                for col_off in range(3):
                    shifted = three_planes[depth_off, row_off:row_off + ROWS, col_off:col_off + COLS, :]
                    summed = summed + jnp.dot(shifted.reshape(ROWS * COLS, C), kernel[9 * depth_off + 3 * row_off + col_off], preferred_element_type=jnp.float32)
        return summed.astype(jnp.bfloat16).reshape(ROWS, COLS, C)

    return lax.map(one_plane, jnp.arange(DEPTH, dtype=jnp.int32))
```

```python
import functools

import jax
import jax.numpy as jnp
from jax import lax
from jax.experimental import pallas as pl
from jax.experimental.pallas import tpu as pltpu
from jax.sharding import PartitionSpec as P

TAPS = 27
BOTH = ("slab", "chan")
VMEM_LIMIT = 24 * 1024 * 1024


def whole_vmem(count):
    return [pl.BlockSpec(memory_space=pltpu.VMEM)] * count


def columns_kernel(volume, low, high, row_low, row_high, columns):
    depth, rows, cols, channels = volume.shape
    position = lax.broadcasted_iota(jnp.int32, (cols, channels), 0)
    for d in range(depth + 2):
        for r in range(rows + 2):
            if r == 0:
                line = row_low[d, 0]
            elif r == rows + 1:
                line = row_high[d, 0]
            elif d == 0:
                line = low[0, r - 1]
            elif d == depth + 1:
                line = high[0, r - 1]
            else:
                line = volume[d - 1, r - 1]
            wide = line.astype(jnp.float32)
            before = jnp.where(position == 0, 0.0, pltpu.roll(wide, 1, 0))
            after = jnp.where(position == cols - 1, 0.0, pltpu.roll(wide, cols - 1, 0))
            shifted = (before.astype(line.dtype), line, after.astype(line.dtype))
            for a in range(3):
                for b in range(3):
                    if 0 <= d - a < depth and 0 <= r - b < rows:
                        start = ((d - a) * rows + (r - b)) * cols
                        for e in range(3):
                            tap = 9 * a + 3 * b + e
                            columns[start : start + cols, tap * channels : (tap + 1) * channels] = shifted[e]


def build_columns(volume, low, high, row_low, row_high):
    depth, rows, cols, channels = volume.shape
    return pl.pallas_call(
        columns_kernel,
        out_shape=jax.ShapeDtypeStruct((depth * rows * cols, TAPS * channels), volume.dtype),
        in_specs=whole_vmem(5),
        out_specs=pl.BlockSpec(memory_space=pltpu.VMEM),
        compiler_params=pltpu.CompilerParams(vmem_limit_bytes=VMEM_LIMIT),
        name="columns",
    )(volume, low, high, row_low, row_high)


def product(columns, kernel_rows):
    return lax.dot_general(
        columns, kernel_rows, (((1,), (1,)), ((), ())), preferred_element_type=jnp.float32
    )


def part_kernel(columns, *refs):
    *pieces, out = refs
    kernel_rows = jnp.concatenate([piece[...] for piece in pieces], axis=0)
    out[...] = product(columns[...], kernel_rows).astype(out.dtype)


def part(columns, *pieces):
    voxels, depth = columns.shape
    width = sum(piece.shape[0] for piece in pieces)
    return pl.pallas_call(
        part_kernel,
        out_shape=jax.ShapeDtypeStruct((voxels, width), columns.dtype),
        in_specs=whole_vmem(1 + len(pieces)),
        out_specs=pl.BlockSpec(memory_space=pltpu.VMEM),
        compiler_params=pltpu.CompilerParams(vmem_limit_bytes=VMEM_LIMIT),
        cost_estimate=pl.CostEstimate(
            flops=2 * voxels * depth * width, bytes_accessed=2 * depth * (voxels + width), transcendentals=0
        ),
        name="part",
    )(columns, *pieces)


def last_kernel(columns, first, second, here, there, out):
    slab = lax.axis_index("slab")
    core = lax.rem(lax.axis_index("chan"), 2)
    kernel_rows = jnp.concatenate([here[...], there[...]], axis=0)
    third = product(columns[...], kernel_rows)
    half = here.shape[0]
    first_sum = first[...].astype(jnp.float32)
    second_sum = second[...].astype(jnp.float32)
    own = first_sum[:, : 2 * half]
    r1, o1 = first_sum[:, 2 * half : 3 * half], first_sum[:, 3 * half :]
    r2, o2 = second_sum[:, :half], second_sum[:, half:]
    d, other_d = third[:, :half], third[:, half:]
    even = core == 0
    across_x = jnp.concatenate([jnp.where(even, r1, o1), jnp.where(even, r2, o2)], axis=1)
    across_y = jnp.concatenate([jnp.where(even, o2, r2), jnp.where(even, o1, r1)], axis=1)
    opposite = jnp.concatenate([jnp.where(even, d, other_d), jnp.where(even, other_d, d)], axis=1)
    blocks = [own, across_x, across_y, opposite]
    odd_x = lax.rem(slab, 2) == 1
    blocks = [jnp.where(odd_x, blocks[j ^ 1], blocks[j]) for j in range(4)]
    odd_y = slab >= 2
    blocks = [jnp.where(odd_y, blocks[j ^ 2], blocks[j]) for j in range(4)]
    out[...] = jnp.concatenate(blocks, axis=1).astype(out.dtype)


def last(columns, first, second, here, there):
    voxels, depth = columns.shape
    width = first.shape[1] + second.shape[1] + here.shape[0] + there.shape[0]
    return pl.pallas_call(
        last_kernel,
        out_shape=jax.ShapeDtypeStruct((voxels, width), columns.dtype),
        in_specs=whole_vmem(5),
        out_specs=pl.BlockSpec(memory_space=pltpu.VMEM),
        compiler_params=pltpu.CompilerParams(vmem_limit_bytes=VMEM_LIMIT),
        cost_estimate=pl.CostEstimate(
            flops=2 * voxels * depth * 2 * here.shape[0],
            bytes_accessed=2 * depth * (voxels + 2 * here.shape[0]),
            transcendentals=0,
        ),
        name="last",
    )(columns, first, second, here, there)


def halo(block, axis, dim):
    count = lax.axis_size(axis)
    forward = [(i, i + 1) for i in range(count - 1)]
    backward = [(target, source) for source, target in forward]
    extent = block.shape[dim]
    low = lax.ppermute(lax.slice_in_dim(block, extent - 1, extent, axis=dim), axis, forward)
    high = lax.ppermute(lax.slice_in_dim(block, 0, 1, axis=dim), axis, backward)
    return low, high


def four_slabs(columns_of, weights):
    chans = lax.axis_size("chan")

    def pairs(even_step, odd_step, core_step=0):
        return [
            (s * chans + c, (s ^ (odd_step if c % 2 else even_step)) * chans + (c ^ core_step))
            for s in range(4)
            for c in range(chans)
        ]

    kernel_rows = weights.T
    half = kernel_rows.shape[0] // 2
    core = lax.rem(lax.axis_index("chan"), 2)
    mine = lax.dynamic_slice_in_dim(kernel_rows, core * half, half, 0)
    rest = lax.dynamic_slice_in_dim(kernel_rows, (1 - core) * half, half, 0)
    r1 = lax.ppermute(mine, BOTH, pairs(1, 2))
    r2 = lax.ppermute(rest, BOTH, pairs(1, 2))
    columns = columns_of()
    d = lax.ppermute(r1, BOTH, pairs(2, 1))
    swap = pairs(0, 0, 1)
    o1 = lax.ppermute(r1, BOTH, swap)
    o2 = lax.ppermute(r2, BOTH, swap)
    other_d = lax.ppermute(d, BOTH, swap)
    first = part(columns, kernel_rows, r1, o1)
    second = part(columns, r2, o2)
    return last(columns, first, second, d, other_d)


def local(volume, weights):
    def columns_of():
        low, high = halo(volume, "slab", 0)
        tall = jnp.concatenate([low, volume, high], axis=0)
        row_low, row_high = halo(tall, "chan", 1)
        return build_columns(volume, low, high, row_low, row_high)

    if lax.axis_size("slab") == 4 and lax.axis_size("chan") % 2 == 0:
        out = four_slabs(columns_of, weights)
    else:
        gathered = lax.all_gather(weights.T, "slab", axis=0, tiled=True)
        out = part(columns_of(), gathered)
    return out.reshape(volume.shape)


def solution(mesh):
    placed = (P("slab", "chan", None, None), P(None, "slab"))
    return jax.shard_map(
        local, mesh=mesh, in_specs=placed, out_specs=P("slab", "chan", None, None), check_vma=False
    )
```

```python
import jax
import jax.numpy as jnp
from jax import lax
from jax.experimental import pallas as pl
from jax.experimental.pallas import tpu as pltpu
from jax.sharding import PartitionSpec as P

BOTH = ("slab", "chan")
VMEM_LIMIT = 24 * 1024 * 1024


def call(kernel, operands, outs, flops=0, places=None, scratch=()):
    size = sum(x.size * x.dtype.itemsize for x in (*operands, *outs))
    vmem = pl.BlockSpec(memory_space=pltpu.VMEM)
    return pl.pallas_call(
        kernel,
        out_shape=outs,
        in_specs=places or [vmem] * len(operands),
        out_specs=[vmem] * len(outs),
        scratch_shapes=scratch,
        compiler_params=pltpu.CompilerParams(vmem_limit_bytes=VMEM_LIMIT),
        cost_estimate=pl.CostEstimate(flops=flops, bytes_accessed=size, transcendentals=0),
        name=kernel.__name__,
    )(*operands)


def like(shape, array):
    return jax.ShapeDtypeStruct(shape, array.dtype)


def core_parity():
    return lax.rem(lax.axis_index("chan"), 2)


def slab_x():
    return lax.rem(lax.axis_index("slab"), 2)


def slab_y():
    return lax.div(lax.axis_index("slab"), 2)


def fetch(volume, kernel_rows, first, second, block, sems):
    count = first.shape[0]
    start = core_parity() * 2 * count
    copies = [
        pltpu.make_async_copy(kernel_rows.at[pl.ds(pl.multiple_of(start, count), count), :], first, sems.at[0]),
        pltpu.make_async_copy(kernel_rows.at[pl.ds(pl.multiple_of(start + count, count), count), :], second, sems.at[1]),
        pltpu.make_async_copy(volume, block, sems.at[2]),
    ]
    for copy in copies:
        copy.start()
    for copy in copies:
        copy.wait()


def border(block, across, out):
    plane = (block.shape[0] - 1) * (1 - slab_y())
    for r in range(block.shape[1]):
        out[0, r] = jnp.where(slab_x() == slab_y(), across[plane, r], block[plane, r])


def edges(block, across, to_core, to_chip):
    depth, rows = block.shape[:2]
    core = core_parity()
    for out, row in ((to_core, (rows - 1) * (1 - core)), (to_chip, (rows - 1) * core)):
        for d in range(depth):
            out[d, 0] = block[d, row]
            out[depth + d, 0] = across[d, row]


def outer_edges(outer, to_core, to_chip):
    rows = outer.shape[1]
    core = core_parity()
    for out, row in ((to_core, (rows - 1) * (1 - core)), (to_chip, (rows - 1) * core)):
        out[0, 0] = outer[0, row]


def extend(block, across, outer, from_core, from_chip, outer_core, outer_chip, lines):
    depth, rows = block.shape[:2]
    even_core = core_parity() == 0
    first, second = depth * slab_x() + 1, depth * (1 - slab_x()) + 1
    beyond = (2 * depth + 1) * (1 - slab_y())
    empty = (2 * depth + 1) * slab_y()
    for d in range(2 * depth + 1):
        if d < depth:
            target, source, core_row, chip_row = first + d, block.at[d], from_core[d, 0], from_chip[d, 0]
        elif d < 2 * depth:
            target, source, core_row, chip_row = second + d - depth, across.at[d - depth], from_core[d, 0], from_chip[d, 0]
        else:
            target, source, core_row, chip_row = beyond, outer.at[0], outer_core[0, 0], outer_chip[0, 0]
        lines[target, 0] = jnp.where(even_core, chip_row, core_row)
        for r in range(rows):
            lines[target, r + 1] = source[r]
        lines[target, rows + 1] = jnp.where(even_core, core_row, chip_row)
    lines[empty] = jnp.zeros(lines.shape[1:], lines.dtype)


def convolve(lines, base, depth, pieces):
    rows, cols, channels = lines.shape[1] - 2, *lines.shape[2:]
    voxels = depth * rows * cols
    width = sum(piece.shape[0] for piece in pieces)
    total = None
    for a in range(3):
        for b in range(3):
            moved = lines[pl.ds(base + a, depth), b : b + rows].reshape(voxels, channels)
            taps = [
                piece[:, (9 * a + 3 * b + e) * channels : (9 * a + 3 * b + e + 1) * channels]
                for e in range(3)
                for piece in pieces
            ]
            term = lax.dot_general(
                moved, jnp.concatenate(taps, axis=0), (((1,), (1,)), ((), ())), preferred_element_type=jnp.float32
            )
            total = term if total is None else total + term
    col = lax.rem(lax.broadcasted_iota(jnp.int32, (voxels, width), 0), cols)
    before = jnp.where(col == 0, 0.0, pltpu.roll(total[:, :width], 1, 0))
    after = jnp.where(col == cols - 1, 0.0, pltpu.roll(total[:, 2 * width :], voxels - 1, 0))
    return before + total[:, width : 2 * width] + after


def ordered(sums):
    half = sums.shape[1] // 2
    swapped = jnp.concatenate([sums[:, half:], sums[:, :half]], axis=1)
    return jnp.where(core_parity() == 0, sums, swapped)


def near(lines, kernel_rows, out):
    depth = (lines.shape[0] - 2) // 2
    out[...] = convolve(lines, depth * (1 - slab_x()), depth, [kernel_rows]).astype(out.dtype)


def back(lines, near_sums, *refs):
    depth = (lines.shape[0] - 2) // 2
    *pieces, out = refs
    sums = ordered(convolve(lines, depth * (1 - slab_x()), depth, pieces))
    out[...] = jnp.concatenate([near_sums[...], sums.astype(out.dtype)], axis=1)


def kept(lines, kernel_rows, *refs):
    depth = (lines.shape[0] - 2) // 2
    *pieces, out = refs
    width = kernel_rows.shape[0]
    sums = convolve(lines, depth * slab_x(), depth, [kernel_rows, *pieces])
    out[...] = jnp.concatenate([sums[:, :width], ordered(sums[:, width:])], axis=1).astype(out.dtype)


def join(kept_sums, returned, out):
    width = kept_sums.shape[1] // 2
    mine, theirs = kept_sums[...].astype(jnp.float32), returned[...].astype(jnp.float32)
    blocks = [mine[:, :width], theirs[:, :width], mine[:, width:], theirs[:, width:]]
    odd_x, odd_y = slab_x() == 1, slab_y() == 1
    blocks = [jnp.where(odd_x, blocks[j ^ 1], blocks[j]) for j in range(4)]
    blocks = [jnp.where(odd_y, blocks[j ^ 2], blocks[j]) for j in range(4)]
    out[...] = jnp.concatenate(blocks, axis=1).astype(out.dtype)


def four_slabs(volume, weights):
    chans = lax.axis_size("chan")
    depth, rows, cols, channels = volume.shape
    voxels = depth * rows * cols
    kernel_rows = weights.T
    width, depth_of_sum = kernel_rows.shape

    def send(array, target):
        every = [(s * chans + c, target(s, c)) for s in range(4) for c in range(chans)]
        pairs = [(source, s * chans + c) for source, (s, c) in every if 0 <= s < 4 and 0 <= c < chans]
        return lax.ppermute(array, BOTH, pairs)

    def across_x(s, c):
        return s ^ 1, c

    def across_y(s, c):
        return s ^ 2, c

    def other_core(s, c):
        return s, c ^ 1

    def next_chip(s, c):
        return s, c + (1 if c % 2 else -1)

    across = send(volume, across_x)
    piece = like((width // 4, depth_of_sum), weights)
    first, second, block = call(
        fetch,
        [pltpu.with_memory_space_constraint(x, pltpu.HBM) for x in (volume, kernel_rows)],
        [piece, piece, like(volume.shape, volume)],
        places=[pl.BlockSpec(memory_space=pltpu.HBM)] * 2,
        scratch=[pltpu.SemaphoreType.DMA((3,))],
    )
    here_first = send(first, across_y)
    second, across = lax.optimization_barrier((second, across))
    (plane,) = call(border, (block, across), [like((1, rows, cols, channels), volume)], 1000000000)
    outer = send(plane, across_y)
    here_second = send(second, across_y)
    edge, outer_edge = like((2 * depth, 1, cols, channels), volume), like((1, 1, cols, channels), volume)
    to_core, to_chip = call(edges, (block, across), [edge, edge])
    from_core, from_chip = send(to_core, other_core), send(to_chip, next_chip)
    outer, here_first = lax.optimization_barrier((outer, here_first))
    to_core, to_chip = call(outer_edges, (outer,), [outer_edge, outer_edge], 3000000000)
    outer_core, outer_chip = send(to_core, other_core), send(to_chip, next_chip)
    (lines,) = call(
        extend,
        (block, across, outer, from_core, from_chip, outer_core, outer_chip),
        [like((2 * depth + 2, rows + 2, cols, channels), volume)],
    )
    work = 2 * voxels * depth_of_sum * width
    (near_sums,) = call(near, (lines, kernel_rows), [like((voxels, width), volume)], work)
    there_first = send(here_first, other_core)
    here_second, held = lax.optimization_barrier((here_second, lines))
    there_second = send(here_second, other_core)
    pieces = (here_first, here_second, there_first, there_second)
    both = like((voxels, 2 * width), volume)
    (sent,) = call(back, (lines, near_sums, *pieces), [both], work)
    returned = send(sent, across_x)
    (mine,) = call(kept, (lines, kernel_rows, *pieces), [both], 2 * work)
    (out,) = call(join, (mine, returned), [like((voxels, 4 * width), volume)])
    return out.reshape(volume.shape)


def halo(block, axis, dim):
    count = lax.axis_size(axis)
    forward = [(i, i + 1) for i in range(count - 1)]
    backward = [(target, source) for source, target in forward]
    extent = block.shape[dim]
    low = lax.ppermute(lax.slice_in_dim(block, extent - 1, extent, axis=dim), axis, forward)
    high = lax.ppermute(lax.slice_in_dim(block, 0, 1, axis=dim), axis, backward)
    return jnp.concatenate([low, block, high], axis=dim)


def whole(lines, kernel_rows, out):
    out[...] = convolve(lines, 0, lines.shape[0] - 2, [kernel_rows]).astype(out.dtype)


def any_slabs(volume, weights):
    gathered = lax.all_gather(weights.T, "slab", axis=0, tiled=True)
    lines = halo(halo(volume, "slab", 0), "chan", 1)
    voxels, (width, depth_of_sum) = volume.size // volume.shape[-1], gathered.shape
    (out,) = call(whole, (lines, gathered), [like((voxels, width), volume)], 2 * voxels * depth_of_sum * width)
    return out.reshape(volume.shape)


def local(volume, weights):
    if lax.axis_size("slab") == 4 and lax.axis_size("chan") % 2 == 0:
        return four_slabs(volume, weights)
    return any_slabs(volume, weights)


def solution(mesh):
    placed = (P("slab", "chan", None, None), P(None, "slab"))
    return jax.shard_map(
        local, mesh=mesh, in_specs=placed, out_specs=P("slab", "chan", None, None), check_vma=False
    )
```

```python
import jax
import jax.numpy as jnp
from jax import lax
from jax.experimental import pallas as pl
from jax.experimental.pallas import tpu as pltpu
from jax.sharding import PartitionSpec as P

BOTH = ("slab", "chan")
VMEM_LIMIT = 24 * 1024 * 1024
EARLY_TAPS = 9


def call(kernel, operands, outs, flops=0, places=None, scratch=()):
    size = sum(x.size * x.dtype.itemsize for x in (*operands, *outs))
    vmem = pl.BlockSpec(memory_space=pltpu.VMEM)
    return pl.pallas_call(
        kernel,
        out_shape=outs,
        in_specs=places or [vmem] * len(operands),
        out_specs=[vmem] * len(outs),
        scratch_shapes=scratch,
        compiler_params=pltpu.CompilerParams(vmem_limit_bytes=VMEM_LIMIT),
        cost_estimate=pl.CostEstimate(flops=flops, bytes_accessed=size, transcendentals=0),
        name=kernel.__name__,
    )(*operands)


def like(shape, array):
    return jax.ShapeDtypeStruct(shape, array.dtype)


def core_parity():
    return lax.rem(lax.axis_index("chan"), 2)


def slab_x():
    return lax.rem(lax.axis_index("slab"), 2)


def slab_y():
    return lax.div(lax.axis_index("slab"), 2)


def fetch(volume, kernel_rows, first, second, block, sems):
    count, early = first.shape
    rows = pl.ds(pl.multiple_of(core_parity() * count, count), count)
    copies = [
        pltpu.make_async_copy(kernel_rows.at[rows, pl.ds(0, early)], first, sems.at[0]),
        pltpu.make_async_copy(kernel_rows.at[rows, pl.ds(early, second.shape[1])], second, sems.at[1]),
        pltpu.make_async_copy(volume, block, sems.at[2]),
    ]
    for copy in copies:
        copy.start()
    for copy in copies:
        copy.wait()


def border(block, across, out):
    plane = (block.shape[0] - 1) * (1 - slab_y())
    for r in range(block.shape[1]):
        out[0, r] = jnp.where(slab_x() == slab_y(), across[plane, r], block[plane, r])


def edges(block, across, to_core, to_chip):
    depth, rows = block.shape[:2]
    core = core_parity()
    for out, row in ((to_core, (rows - 1) * (1 - core)), (to_chip, (rows - 1) * core)):
        for d in range(depth):
            out[d, 0] = block[d, row]
            out[depth + d, 0] = across[d, row]


def outer_edges(outer, to_core, to_chip):
    rows = outer.shape[1]
    core = core_parity()
    for out, row in ((to_core, (rows - 1) * (1 - core)), (to_chip, (rows - 1) * core)):
        out[0, 0] = outer[0, row]


def extend(block, across, outer, from_core, from_chip, outer_core, outer_chip, lines):
    depth, rows = block.shape[:2]
    even_core = core_parity() == 0
    first, second = depth * slab_x() + 1, depth * (1 - slab_x()) + 1
    beyond = (2 * depth + 1) * (1 - slab_y())
    empty = (2 * depth + 1) * slab_y()
    for d in range(2 * depth + 1):
        if d < depth:
            target, source, core_row, chip_row = first + d, block.at[d], from_core[d, 0], from_chip[d, 0]
        elif d < 2 * depth:
            target, source, core_row, chip_row = second + d - depth, across.at[d - depth], from_core[d, 0], from_chip[d, 0]
        else:
            target, source, core_row, chip_row = beyond, outer.at[0], outer_core[0, 0], outer_chip[0, 0]
        lines[target, 0] = jnp.where(even_core, chip_row, core_row)
        for r in range(rows):
            lines[target, r + 1] = source[r]
        lines[target, rows + 1] = jnp.where(even_core, core_row, chip_row)
    lines[empty] = jnp.zeros(lines.shape[1:], lines.dtype)


def convolve(lines, base, depth, kernel_rows, pieces):
    rows, cols, channels = lines.shape[1] - 2, *lines.shape[2:]
    voxels = depth * rows * cols
    total = None
    for tap in range(0, 27, 3):
        a, b = tap // 9, tap // 3 % 3
        moved = lines[pl.ds(base + a, depth), b : b + rows].reshape(voxels, channels)
        stack = []
        for e in range(3):
            at = (tap + e) * channels
            stack.append(kernel_rows[:, at : at + channels])
            for first, second in pieces:
                early = first.shape[1]
                array, start = (first, at) if at < early else (second, at - early)
                stack.append(array[:, start : start + channels])
        term = lax.dot_general(
            moved, jnp.concatenate(stack, axis=0), (((1,), (1,)), ((), ())), preferred_element_type=jnp.float32
        )
        total = term if total is None else total + term
    width = total.shape[1] // 3
    col = lax.rem(lax.broadcasted_iota(jnp.int32, (voxels, width), 0), cols)
    before = jnp.where(col == 0, 0.0, pltpu.roll(total[:, :width], 1, 0))
    after = jnp.where(col == cols - 1, 0.0, pltpu.roll(total[:, 2 * width :], voxels - 1, 0))
    return before + total[:, width : 2 * width] + after


def ordered(sums):
    half = sums.shape[1] // 2
    swapped = jnp.concatenate([sums[:, half:], sums[:, :half]], axis=1)
    return jnp.where(core_parity() == 0, sums, swapped)


def both_slabs(lines, base, kernel_rows, pieces, out):
    width = kernel_rows.shape[0]
    here_first, here_second, there_first, there_second = pieces
    pieces = ((here_first, here_second), (there_first, there_second))
    sums = convolve(lines, base, (lines.shape[0] - 2) // 2, kernel_rows, pieces)
    near, far = sums[:, :width], ordered(sums[:, width:])
    even = jnp.concatenate([near, far], axis=1)
    out[...] = jnp.where(slab_x() == 0, even, jnp.concatenate([far, near], axis=1)).astype(out.dtype)


def back(lines, kernel_rows, *refs):
    *pieces, out = refs
    both_slabs(lines, (lines.shape[0] - 2) // 2 * (1 - slab_x()), kernel_rows, pieces, out)


def kept(lines, kernel_rows, *refs):
    *pieces, out = refs
    both_slabs(lines, (lines.shape[0] - 2) // 2 * slab_x(), kernel_rows, pieces, out)


def join(kept_sums, returned, out):
    voxels, width = kept_sums.shape
    mine, theirs = kept_sums[...].astype(jnp.float32), returned[...].astype(jnp.float32)
    here = lax.div(lax.broadcasted_iota(jnp.int32, (voxels, width), 1), width // 2) == slab_x()
    near, far = jnp.where(here, mine, theirs), jnp.where(here, theirs, mine)
    near_at = pl.multiple_of(slab_y() * width, width)
    far_at = pl.multiple_of((1 - slab_y()) * width, width)
    out[:, pl.ds(near_at, width)] = near.astype(out.dtype)
    out[:, pl.ds(far_at, width)] = pltpu.roll(far, width // 2, 1).astype(out.dtype)


def four_slabs(volume, weights):
    chans = lax.axis_size("chan")
    depth, rows, cols, channels = volume.shape
    voxels = depth * rows * cols
    kernel_rows = weights.T
    width, depth_of_sum = kernel_rows.shape

    def send(array, target):
        every = [(s * chans + c, target(s, c)) for s in range(4) for c in range(chans)]
        pairs = [(source, s * chans + c) for source, (s, c) in every if 0 <= s < 4 and 0 <= c < chans]
        return lax.ppermute(array, BOTH, pairs)

    def across_x(s, c):
        return s ^ 1, c

    def across_y(s, c):
        return s ^ 2, c

    def other_core(s, c):
        return s, c ^ 1

    def next_chip(s, c):
        return s, c + (1 if c % 2 else -1)

    across = send(volume, across_x)
    early = EARLY_TAPS * channels
    pieces = [like((width // 2, early), weights), like((width // 2, depth_of_sum - early), weights)]
    first, second, block = call(
        fetch,
        [pltpu.with_memory_space_constraint(x, pltpu.HBM) for x in (volume, kernel_rows)],
        [*pieces, like(volume.shape, volume)],
        places=[pl.BlockSpec(memory_space=pltpu.HBM)] * 2,
        scratch=[pltpu.SemaphoreType.DMA((3,))],
    )
    here_first = send(first, across_y)
    second, across = lax.optimization_barrier((second, across))
    (plane,) = call(border, (block, across), [like((1, rows, cols, channels), volume)], 1000000000)
    outer = send(plane, across_y)
    here_second = send(second, across_y)
    edge, outer_edge = like((2 * depth, 1, cols, channels), volume), like((1, 1, cols, channels), volume)
    to_core, to_chip = call(edges, (block, across), [edge, edge])
    from_core, from_chip = send(to_core, other_core), send(to_chip, next_chip)
    outer, here_first = lax.optimization_barrier((outer, here_first))
    to_core, to_chip = call(outer_edges, (outer,), [outer_edge, outer_edge], 3000000000)
    outer_core, outer_chip = send(to_core, other_core), send(to_chip, next_chip)
    there_first = send(here_first, other_core)
    here_second, outer_core = lax.optimization_barrier((here_second, outer_core))
    there_second = send(here_second, other_core)
    (lines,) = call(
        extend,
        (block, across, outer, from_core, from_chip, outer_core, outer_chip),
        [like((2 * depth + 2, rows + 2, cols, channels), volume)],
        3000000000,
    )
    work = 2 * voxels * depth_of_sum * width
    pieces = (here_first, here_second, there_first, there_second)
    both = like((voxels, 2 * width), volume)
    (sent,) = call(back, (lines, kernel_rows, *pieces), [both], 2 * work)
    returned = send(sent, across_x)
    (mine,) = call(kept, (lines, kernel_rows, *pieces), [both], 2 * work)
    (out,) = call(join, (mine, returned), [like((voxels, 4 * width), volume)])
    return out.reshape(volume.shape)


def halo(block, axis, dim):
    count = lax.axis_size(axis)
    forward = [(i, i + 1) for i in range(count - 1)]
    backward = [(target, source) for source, target in forward]
    extent = block.shape[dim]
    low = lax.ppermute(lax.slice_in_dim(block, extent - 1, extent, axis=dim), axis, forward)
    high = lax.ppermute(lax.slice_in_dim(block, 0, 1, axis=dim), axis, backward)
    return jnp.concatenate([low, block, high], axis=dim)


def whole(lines, kernel_rows, out):
    out[...] = convolve(lines, 0, lines.shape[0] - 2, kernel_rows, ()).astype(out.dtype)


def any_slabs(volume, weights):
    gathered = lax.all_gather(weights.T, "slab", axis=0, tiled=True)
    lines = halo(halo(volume, "slab", 0), "chan", 1)
    voxels, (width, depth_of_sum) = volume.size // volume.shape[-1], gathered.shape
    (out,) = call(whole, (lines, gathered), [like((voxels, width), volume)], 2 * voxels * depth_of_sum * width)
    return out.reshape(volume.shape)


def local(volume, weights):
    if lax.axis_size("slab") == 4 and lax.axis_size("chan") % 2 == 0:
        return four_slabs(volume, weights)
    return any_slabs(volume, weights)


def solution(mesh):
    placed = (P("slab", "chan", None, None), P(None, "slab"))
    return jax.shard_map(
        local, mesh=mesh, in_specs=placed, out_specs=P("slab", "chan", None, None), check_vma=False
    )
```

```python
import jax
import jax.numpy as jnp
from jax import lax
from jax.experimental import pallas as pl
from jax.experimental.pallas import tpu as pltpu
from jax.sharding import PartitionSpec as P

BOTH = ("slab", "chan")
VMEM_LIMIT = 24 * 1024 * 1024
EARLY_TAPS = 9


def call(kernel, operands, outs, flops=0, places=None, scratch=()):
    size = sum(x.size * x.dtype.itemsize for x in (*operands, *outs))
    vmem = pl.BlockSpec(memory_space=pltpu.VMEM)
    return pl.pallas_call(
        kernel,
        out_shape=outs,
        in_specs=places or [vmem] * len(operands),
        out_specs=[vmem] * len(outs),
        scratch_shapes=scratch,
        compiler_params=pltpu.CompilerParams(vmem_limit_bytes=VMEM_LIMIT),
        cost_estimate=pl.CostEstimate(flops=flops, bytes_accessed=size, transcendentals=0),
        name=kernel.__name__,
    )(*operands)


def like(shape, array):
    return jax.ShapeDtypeStruct(shape, array.dtype)


def core_parity():
    return lax.rem(lax.axis_index("chan"), 2)


def slab_x():
    return lax.rem(lax.axis_index("slab"), 2)


def slab_y():
    return lax.div(lax.axis_index("slab"), 2)


def fetch(volume, kernel_rows, first, second, block, sems):
    count, early = first.shape
    rows = pl.ds(pl.multiple_of(core_parity() * count, count), count)
    copies = [
        pltpu.make_async_copy(kernel_rows.at[rows, pl.ds(0, early)], first, sems.at[0]),
        pltpu.make_async_copy(kernel_rows.at[rows, pl.ds(early, second.shape[1])], second, sems.at[1]),
        pltpu.make_async_copy(volume, block, sems.at[2]),
    ]
    for copy in copies:
        copy.start()
    for copy in copies:
        copy.wait()


def border(block, across, out):
    plane = (block.shape[0] - 1) * (1 - slab_y())
    for r in range(block.shape[1]):
        out[0, r] = jnp.where(slab_x() == slab_y(), across[plane, r], block[plane, r])


def edges(block, across, to_core, to_chip):
    depth, rows = block.shape[:2]
    core = core_parity()
    for out, row in ((to_core, (rows - 1) * (1 - core)), (to_chip, (rows - 1) * core)):
        for d in range(depth):
            out[d, 0] = block[d, row]
            out[depth + d, 0] = across[d, row]


def outer_edges(outer, to_core, to_chip):
    rows = outer.shape[1]
    core = core_parity()
    for out, row in ((to_core, (rows - 1) * (1 - core)), (to_chip, (rows - 1) * core)):
        out[0, 0] = outer[0, row]


def extend(block, across, outer, from_core, from_chip, outer_core, outer_chip, lines):
    depth, rows = block.shape[:2]
    even_core = core_parity() == 0
    first, second = depth * slab_x() + 1, depth * (1 - slab_x()) + 1
    beyond = (2 * depth + 1) * (1 - slab_y())
    empty = (2 * depth + 1) * slab_y()
    for d in range(2 * depth + 1):
        if d < depth:
            target, source, core_row, chip_row = first + d, block.at[d], from_core[d, 0], from_chip[d, 0]
        elif d < 2 * depth:
            target, source, core_row, chip_row = second + d - depth, across.at[d - depth], from_core[d, 0], from_chip[d, 0]
        else:
            target, source, core_row, chip_row = beyond, outer.at[0], outer_core[0, 0], outer_chip[0, 0]
        lines[target, 0] = jnp.where(even_core, chip_row, core_row)
        for r in range(rows):
            lines[target, r + 1] = source[r]
        lines[target, rows + 1] = jnp.where(even_core, core_row, chip_row)
    lines[empty] = jnp.zeros(lines.shape[1:], lines.dtype)


def convolve(lines, base, depth, groups):
    rows, cols, channels = lines.shape[1] - 2, *lines.shape[2:]
    voxels = depth * rows * cols
    total = None
    for taps, arrays in groups:
        for tap in taps[::3]:
            a, b, start = tap // 9, tap // 3 % 3, (tap - taps[0]) * channels
            moved = lines[pl.ds(base + a, depth), b : b + rows].reshape(voxels, channels)
            stack = [
                array[:, start + e * channels : start + (e + 1) * channels] for e in range(3) for array in arrays
            ]
            term = lax.dot_general(
                moved, jnp.concatenate(stack, axis=0), (((1,), (1,)), ((), ())), preferred_element_type=jnp.float32
            )
            total = term if total is None else total + term
    width = total.shape[1] // 3
    col = lax.rem(lax.broadcasted_iota(jnp.int32, (voxels, width), 0), cols)
    before = jnp.where(col == 0, 0.0, pltpu.roll(total[:, :width], 1, 0))
    after = jnp.where(col == cols - 1, 0.0, pltpu.roll(total[:, 2 * width :], voxels - 1, 0))
    return before + total[:, width : 2 * width] + after


def ordered(sums):
    half = sums.shape[1] // 2
    swapped = jnp.concatenate([sums[:, half:], sums[:, :half]], axis=1)
    return jnp.where(core_parity() == 0, sums, swapped)


def pair_depth(lines):
    return (lines.shape[0] - 2) // 2


def arranged(near, far):
    far = ordered(far)
    return jnp.where(slab_x() == 0, jnp.concatenate([near, far], axis=1), jnp.concatenate([far, near], axis=1))


def back_early(lines, kernel_rows, here, there, near, far):
    depth, early = pair_depth(lines), here.shape[1] // lines.shape[3]
    base = depth * (1 - slab_x())
    near[...] = convolve(lines, base, depth, [(range(27), [kernel_rows])])
    far[...] = convolve(lines, base, depth, [(range(early), [here, there])])


def back(lines, near, far, here, there, out):
    depth, late = pair_depth(lines), here.shape[1] // lines.shape[3]
    rest = convolve(lines, depth * (1 - slab_x()), depth, [(range(27 - late, 27), [here, there])])
    out[...] = arranged(near[...], far[...] + rest).astype(out.dtype)


def kept(lines, kernel_rows, here_first, there_first, here_second, there_second, out):
    depth, early = pair_depth(lines), here_first.shape[1] // lines.shape[3]
    base, width = depth * slab_x(), kernel_rows.shape[0]
    near = convolve(lines, base, depth, [(range(27), [kernel_rows])])
    groups = [(range(early), [here_first, there_first]), (range(early, 27), [here_second, there_second])]
    out[...] = arranged(near, convolve(lines, base, depth, groups)).astype(out.dtype)


def join(kept_sums, returned, out):
    voxels, width = kept_sums.shape
    mine, theirs = kept_sums[...].astype(jnp.float32), returned[...].astype(jnp.float32)
    here = lax.div(lax.broadcasted_iota(jnp.int32, (voxels, width), 1), width // 2) == slab_x()
    near, far = jnp.where(here, mine, theirs), jnp.where(here, theirs, mine)
    near_at = pl.multiple_of(slab_y() * width, width)
    far_at = pl.multiple_of((1 - slab_y()) * width, width)
    out[:, pl.ds(near_at, width)] = near.astype(out.dtype)
    out[:, pl.ds(far_at, width)] = pltpu.roll(far, width // 2, 1).astype(out.dtype)


def four_slabs(volume, weights):
    chans = lax.axis_size("chan")
    depth, rows, cols, channels = volume.shape
    voxels = depth * rows * cols
    kernel_rows = weights.T
    width, depth_of_sum = kernel_rows.shape

    def send(array, target):
        every = [(s * chans + c, target(s, c)) for s in range(4) for c in range(chans)]
        pairs = [(source, s * chans + c) for source, (s, c) in every if 0 <= s < 4 and 0 <= c < chans]
        return lax.ppermute(array, BOTH, pairs)

    def across_x(s, c):
        return s ^ 1, c

    def across_y(s, c):
        return s ^ 2, c

    def other_core(s, c):
        return s, c ^ 1

    def next_chip(s, c):
        return s, c + (1 if c % 2 else -1)

    across = send(volume, across_x)
    early = EARLY_TAPS * channels
    pieces = [like((width // 2, early), weights), like((width // 2, depth_of_sum - early), weights)]
    first, second, block = call(
        fetch,
        [pltpu.with_memory_space_constraint(x, pltpu.HBM) for x in (volume, kernel_rows)],
        [*pieces, like(volume.shape, volume)],
        places=[pl.BlockSpec(memory_space=pltpu.HBM)] * 2,
        scratch=[pltpu.SemaphoreType.DMA((3,))],
    )
    here_first = send(first, across_y)
    second, across = lax.optimization_barrier((second, across))
    (plane,) = call(border, (block, across), [like((1, rows, cols, channels), volume)], 1000000000)
    outer = send(plane, across_y)
    here_second = send(second, across_y)
    edge, outer_edge = like((2 * depth, 1, cols, channels), volume), like((1, 1, cols, channels), volume)
    to_core, to_chip = call(edges, (block, across), [edge, edge], 5000000000)
    from_core, from_chip = send(to_core, other_core), send(to_chip, next_chip)
    outer, here_first = lax.optimization_barrier((outer, here_first))
    to_core, to_chip = call(outer_edges, (outer,), [outer_edge, outer_edge], 8000000000)
    outer_core, outer_chip = send(to_core, other_core), send(to_chip, next_chip)
    here_first, to_chip_held = lax.optimization_barrier((here_first, outer_core))
    there_first = send(here_first, other_core)
    here_second, outer_core = lax.optimization_barrier((here_second, outer_core))
    there_second = send(here_second, other_core)
    (lines,) = call(
        extend,
        (block, across, outer, from_core, from_chip, outer_core, outer_chip),
        [like((2 * depth + 2, rows + 2, cols, channels), volume)],
        3000000000,
    )
    work = 2 * voxels * depth_of_sum * width
    both, sums = like((voxels, 2 * width), volume), jax.ShapeDtypeStruct((voxels, width), jnp.float32)
    near, far = call(back_early, (lines, kernel_rows, here_first, there_first), [sums, sums], work)
    (sent,) = call(back, (lines, near, far, here_second, there_second), [both], work)
    returned = send(sent, across_x)
    (mine,) = call(
        kept, (lines, kernel_rows, here_first, there_first, here_second, there_second), [both], 2 * work
    )
    (out,) = call(join, (mine, returned), [like((voxels, 4 * width), volume)])
    return out.reshape(volume.shape)


def halo(block, axis, dim):
    count = lax.axis_size(axis)
    forward = [(i, i + 1) for i in range(count - 1)]
    backward = [(target, source) for source, target in forward]
    extent = block.shape[dim]
    low = lax.ppermute(lax.slice_in_dim(block, extent - 1, extent, axis=dim), axis, forward)
    high = lax.ppermute(lax.slice_in_dim(block, 0, 1, axis=dim), axis, backward)
    return jnp.concatenate([low, block, high], axis=dim)


def whole(lines, kernel_rows, out):
    out[...] = convolve(lines, 0, lines.shape[0] - 2, [(range(27), [kernel_rows])]).astype(out.dtype)


def any_slabs(volume, weights):
    gathered = lax.all_gather(weights.T, "slab", axis=0, tiled=True)
    lines = halo(halo(volume, "slab", 0), "chan", 1)
    voxels, (width, depth_of_sum) = volume.size // volume.shape[-1], gathered.shape
    (out,) = call(whole, (lines, gathered), [like((voxels, width), volume)], 2 * voxels * depth_of_sum * width)
    return out.reshape(volume.shape)


def local(volume, weights):
    if lax.axis_size("slab") == 4 and lax.axis_size("chan") % 2 == 0:
        return four_slabs(volume, weights)
    return any_slabs(volume, weights)


def solution(mesh):
    placed = (P("slab", "chan", None, None), P(None, "slab"))
    return jax.shard_map(
        local, mesh=mesh, in_specs=placed, out_specs=P("slab", "chan", None, None), check_vma=False
    )
```

```python
import jax
import jax.numpy as jnp
from jax import lax
from jax.experimental import pallas as pl
from jax.experimental.pallas import tpu as pltpu
from jax.sharding import PartitionSpec as P

BOTH = ("slab", "chan")
VMEM_LIMIT = 24 * 1024 * 1024
EARLY_TAPS = 9
BORDER_COST, OUTER_EDGE_COST, EXTEND_COST = 10**9, 3 * 10**9, 3 * 10**9


def call(kernel, operands, outs, flops=0, places=None, scratch=()):
    size = sum(x.size * x.dtype.itemsize for x in (*operands, *outs))
    vmem = pl.BlockSpec(memory_space=pltpu.VMEM)
    return pl.pallas_call(
        kernel,
        out_shape=outs,
        in_specs=places or [vmem] * len(operands),
        out_specs=[vmem] * len(outs),
        scratch_shapes=scratch,
        compiler_params=pltpu.CompilerParams(vmem_limit_bytes=VMEM_LIMIT),
        cost_estimate=pl.CostEstimate(flops=flops, bytes_accessed=size, transcendentals=0),
        name=kernel.__name__,
    )(*operands)


def like(shape, array):
    return jax.ShapeDtypeStruct(shape, array.dtype)


def core_parity():
    return lax.rem(lax.axis_index("chan"), 2)


def slab_x():
    return lax.rem(lax.axis_index("slab"), 2)


def slab_y():
    return lax.div(lax.axis_index("slab"), 2)


def fetch(volume, kernel_rows, first, second, block, sems):
    count, early = first.shape
    rows = pl.ds(pl.multiple_of(core_parity() * count, count), count)
    copies = [
        pltpu.make_async_copy(kernel_rows.at[rows, pl.ds(0, early)], first, sems.at[0]),
        pltpu.make_async_copy(kernel_rows.at[rows, pl.ds(early, second.shape[1])], second, sems.at[1]),
        pltpu.make_async_copy(volume, block, sems.at[2]),
    ]
    for copy in copies:
        copy.start()
    for copy in copies:
        copy.wait()


def border(block, across, out):
    plane = (block.shape[0] - 1) * (1 - slab_y())
    for r in range(block.shape[1]):
        out[0, r] = jnp.where(slab_x() == slab_y(), across[plane, r], block[plane, r])


def edges(block, across, to_core, to_chip):
    depth, rows = block.shape[:2]
    core = core_parity()
    for out, row in ((to_core, (rows - 1) * (1 - core)), (to_chip, (rows - 1) * core)):
        for d in range(depth):
            out[d, 0] = block[d, row]
            out[depth + d, 0] = across[d, row]


def outer_edge(outer, to_core):
    to_core[0, 0] = outer[0, (outer.shape[1] - 1) * (1 - core_parity())]


def extend(block, across, outer, from_core, from_chip, outer_core, outer_chip, lines):
    depth, rows = block.shape[:2]
    even_core = core_parity() == 0
    first, second = depth * slab_x() + 1, depth * (1 - slab_x()) + 1
    beyond = (2 * depth + 1) * (1 - slab_y())
    empty = (2 * depth + 1) * slab_y()
    for d in range(2 * depth + 1):
        if d < depth:
            target, source, core_row, chip_row = first + d, block.at[d], from_core[d, 0], from_chip[d, 0]
        elif d < 2 * depth:
            target, source, core_row, chip_row = second + d - depth, across.at[d - depth], from_core[d, 0], from_chip[d, 0]
        else:
            target, source = beyond, outer.at[0]
            core_row, chip_row = outer_core[0, 0], outer_chip[0, (rows - 1) * (1 - core_parity())]
        lines[target, 0] = jnp.where(even_core, chip_row, core_row)
        for r in range(rows):
            lines[target, r + 1] = source[r]
        lines[target, rows + 1] = jnp.where(even_core, core_row, chip_row)
    lines[empty] = jnp.zeros(lines.shape[1:], lines.dtype)


def convolve(lines, base, depth, groups):
    rows, cols, channels = lines.shape[1] - 2, *lines.shape[2:]
    voxels = depth * rows * cols
    total = None
    for taps, arrays in groups:
        for tap in taps[::3]:
            a, b, start = tap // 9, tap // 3 % 3, (tap - taps[0]) * channels
            moved = lines[pl.ds(base + a, depth), b : b + rows].reshape(voxels, channels)
            stack = [
                array[:, start + e * channels : start + (e + 1) * channels] for e in range(3) for array in arrays
            ]
            term = lax.dot_general(
                moved, jnp.concatenate(stack, axis=0), (((1,), (1,)), ((), ())), preferred_element_type=jnp.float32
            )
            total = term if total is None else total + term
    width = total.shape[1] // 3
    col = lax.rem(lax.broadcasted_iota(jnp.int32, (voxels, width), 0), cols)
    before = jnp.where(col == 0, 0.0, pltpu.roll(total[:, :width], 1, 0))
    after = jnp.where(col == cols - 1, 0.0, pltpu.roll(total[:, 2 * width :], voxels - 1, 0))
    return before + total[:, width : 2 * width] + after


def ordered(sums):
    half = sums.shape[1] // 2
    swapped = jnp.concatenate([sums[:, half:], sums[:, :half]], axis=1)
    return jnp.where(core_parity() == 0, sums, swapped)


def pair_depth(lines):
    return (lines.shape[0] - 2) // 2


def arranged(near, far):
    far = ordered(far)
    return jnp.where(slab_x() == 0, jnp.concatenate([near, far], axis=1), jnp.concatenate([far, near], axis=1))


def back_early(lines, kernel_rows, here, there, near, far):
    depth, early = pair_depth(lines), here.shape[1] // lines.shape[3]
    base = depth * (1 - slab_x())
    near[...] = convolve(lines, base, depth, [(range(27), [kernel_rows])])
    far[...] = convolve(lines, base, depth, [(range(early), [here, there])])


def back(lines, near, far, here, there, out):
    depth, late = pair_depth(lines), here.shape[1] // lines.shape[3]
    rest = convolve(lines, depth * (1 - slab_x()), depth, [(range(27 - late, 27), [here, there])])
    out[...] = arranged(near[...], far[...] + rest).astype(out.dtype)


def kept(lines, kernel_rows, here_first, there_first, here_second, there_second, out):
    depth, early = pair_depth(lines), here_first.shape[1] // lines.shape[3]
    base, width = depth * slab_x(), kernel_rows.shape[0]
    near = convolve(lines, base, depth, [(range(27), [kernel_rows])])
    groups = [(range(early), [here_first, there_first]), (range(early, 27), [here_second, there_second])]
    out[...] = arranged(near, convolve(lines, base, depth, groups)).astype(out.dtype)


def join(kept_sums, returned, out):
    voxels, width = kept_sums.shape
    mine, theirs = kept_sums[...].astype(jnp.float32), returned[...].astype(jnp.float32)
    here = lax.div(lax.broadcasted_iota(jnp.int32, (voxels, width), 1), width // 2) == slab_x()
    near, far = jnp.where(here, mine, theirs), jnp.where(here, theirs, mine)
    near_at = pl.multiple_of(slab_y() * width, width)
    far_at = pl.multiple_of((1 - slab_y()) * width, width)
    out[:, pl.ds(near_at, width)] = near.astype(out.dtype)
    out[:, pl.ds(far_at, width)] = pltpu.roll(far, width // 2, 1).astype(out.dtype)


def four_slabs(volume, weights):
    chans = lax.axis_size("chan")
    depth, rows, cols, channels = volume.shape
    voxels = depth * rows * cols
    kernel_rows = weights.T
    width, depth_of_sum = kernel_rows.shape

    def send(array, target):
        every = [(s * chans + c, target(s, c)) for s in range(4) for c in range(chans)]
        pairs = [(source, s * chans + c) for source, (s, c) in every if 0 <= s < 4 and 0 <= c < chans]
        return lax.ppermute(array, BOTH, pairs)

    def across_x(s, c):
        return s ^ 1, c

    def across_y(s, c):
        return s ^ 2, c

    def other_core(s, c):
        return s, c ^ 1

    def next_chip(s, c):
        return s, c + (1 if c % 2 else -1)

    across = send(volume, across_x)
    early = EARLY_TAPS * channels
    pieces = [like((width // 2, early), weights), like((width // 2, depth_of_sum - early), weights)]
    first, second, block = call(
        fetch,
        [pltpu.with_memory_space_constraint(x, pltpu.HBM) for x in (volume, kernel_rows)],
        [*pieces, like(volume.shape, volume)],
        places=[pl.BlockSpec(memory_space=pltpu.HBM)] * 2,
        scratch=[pltpu.SemaphoreType.DMA((3,))],
    )
    here_first = send(first, across_y)
    second, across = lax.optimization_barrier((second, across))
    (plane,) = call(border, (block, across), [like((1, rows, cols, channels), volume)], BORDER_COST)
    outer = send(plane, across_y)
    here_second = send(second, across_y)
    edge, line = like((2 * depth, 1, cols, channels), volume), like((1, 1, cols, channels), volume)
    to_core, to_chip = call(edges, (block, across), [edge, edge])
    from_core, from_chip = send(to_core, other_core), send(to_chip, next_chip)
    outer, here_first = lax.optimization_barrier((outer, here_first))
    outer_chip = send(outer, next_chip)
    (to_core,) = call(outer_edge, (outer,), [line], OUTER_EDGE_COST)
    outer_core = send(to_core, other_core)
    here_first, outer_core = lax.optimization_barrier((here_first, outer_core))
    there_first = send(here_first, other_core)
    here_second, outer_core = lax.optimization_barrier((here_second, outer_core))
    there_second = send(here_second, other_core)
    (lines,) = call(
        extend,
        (block, across, outer, from_core, from_chip, outer_core, outer_chip),
        [like((2 * depth + 2, rows + 2, cols, channels), volume)],
        EXTEND_COST,
    )
    work = 2 * voxels * depth_of_sum * width
    both, sums = like((voxels, 2 * width), volume), jax.ShapeDtypeStruct((voxels, width), jnp.float32)
    near, far = call(back_early, (lines, kernel_rows, here_first, there_first), [sums, sums], work)
    (sent,) = call(back, (lines, near, far, here_second, there_second), [both], work)
    returned = send(sent, across_x)
    (mine,) = call(
        kept, (lines, kernel_rows, here_first, there_first, here_second, there_second), [both], 2 * work
    )
    (out,) = call(join, (mine, returned), [like((voxels, 4 * width), volume)])
    return out.reshape(volume.shape)


def halo(block, axis, dim):
    count = lax.axis_size(axis)
    forward = [(i, i + 1) for i in range(count - 1)]
    backward = [(target, source) for source, target in forward]
    extent = block.shape[dim]
    low = lax.ppermute(lax.slice_in_dim(block, extent - 1, extent, axis=dim), axis, forward)
    high = lax.ppermute(lax.slice_in_dim(block, 0, 1, axis=dim), axis, backward)
    return jnp.concatenate([low, block, high], axis=dim)


def whole(lines, kernel_rows, out):
    out[...] = convolve(lines, 0, lines.shape[0] - 2, [(range(27), [kernel_rows])]).astype(out.dtype)


def any_slabs(volume, weights):
    gathered = lax.all_gather(weights.T, "slab", axis=0, tiled=True)
    lines = halo(halo(volume, "slab", 0), "chan", 1)
    voxels, (width, depth_of_sum) = volume.size // volume.shape[-1], gathered.shape
    (out,) = call(whole, (lines, gathered), [like((voxels, width), volume)], 2 * voxels * depth_of_sum * width)
    return out.reshape(volume.shape)


def local(volume, weights):
    if lax.axis_size("slab") == 4 and lax.axis_size("chan") % 2 == 0:
        return four_slabs(volume, weights)
    return any_slabs(volume, weights)


def solution(mesh):
    placed = (P("slab", "chan", None, None), P(None, "slab"))
    return jax.shard_map(
        local, mesh=mesh, in_specs=placed, out_specs=P("slab", "chan", None, None), check_vma=False
    )
```

```python
import jax
import jax.numpy as jnp
from jax import lax
from jax.experimental import pallas as pl
from jax.experimental.pallas import tpu as pltpu
from jax.sharding import PartitionSpec as P

BOTH = ("slab", "chan")
VMEM_LIMIT = 24 * 1024 * 1024
EARLY_TAPS = 9
BORDER_COST, EDGES_COST, OUTER_EDGES_COST, EXTEND_COST = 10**9, 5 * 10**9, 8 * 10**9, 3 * 10**9


def call(kernel, operands, outs, flops=0, places=None, scratch=()):
    size = sum(x.size * x.dtype.itemsize for x in (*operands, *outs))
    vmem = pl.BlockSpec(memory_space=pltpu.VMEM)
    return pl.pallas_call(
        kernel,
        out_shape=outs,
        in_specs=places or [vmem] * len(operands),
        out_specs=[vmem] * len(outs),
        scratch_shapes=scratch,
        compiler_params=pltpu.CompilerParams(vmem_limit_bytes=VMEM_LIMIT),
        cost_estimate=pl.CostEstimate(flops=flops, bytes_accessed=size, transcendentals=0),
        name=kernel.__name__,
    )(*operands)


def like(shape, array):
    return jax.ShapeDtypeStruct(shape, array.dtype)


def core_parity():
    return lax.rem(lax.axis_index("chan"), 2)


def slab_x():
    return lax.rem(lax.axis_index("slab"), 2)


def slab_y():
    return lax.div(lax.axis_index("slab"), 2)


def fetch(volume, kernel_rows, first, second, block, sems):
    count, early = first.shape
    rows = pl.ds(pl.multiple_of(core_parity() * count, count), count)
    copies = [
        pltpu.make_async_copy(kernel_rows.at[rows, pl.ds(0, early)], first, sems.at[0]),
        pltpu.make_async_copy(kernel_rows.at[rows, pl.ds(early, second.shape[1])], second, sems.at[1]),
        pltpu.make_async_copy(volume, block, sems.at[2]),
    ]
    for copy in copies:
        copy.start()
    for copy in copies:
        copy.wait()


def border(block, across, out):
    plane = (block.shape[0] - 1) * (1 - slab_y())
    for r in range(block.shape[1]):
        out[0, r] = jnp.where(slab_x() == slab_y(), across[plane, r], block[plane, r])


def edges(block, across, to_core, to_chip):
    depth, rows = block.shape[:2]
    core = core_parity()
    for out, row in ((to_core, (rows - 1) * (1 - core)), (to_chip, (rows - 1) * core)):
        for d in range(depth):
            out[d, 0] = block[d, row]
            out[depth + d, 0] = across[d, row]


def outer_edges(outer, to_core, to_chip):
    rows = outer.shape[1]
    core = core_parity()
    for out, row in ((to_core, (rows - 1) * (1 - core)), (to_chip, (rows - 1) * core)):
        out[0, 0] = outer[0, row]


def extend(block, across, outer, from_core, from_chip, outer_core, outer_chip, lines):
    depth, rows = block.shape[:2]
    even_core = core_parity() == 0
    first, second = depth * slab_x() + 1, depth * (1 - slab_x()) + 1
    beyond = (2 * depth + 1) * (1 - slab_y())
    empty = (2 * depth + 1) * slab_y()
    for d in range(2 * depth + 1):
        if d < depth:
            target, source, core_row, chip_row = first + d, block.at[d], from_core[d, 0], from_chip[d, 0]
        elif d < 2 * depth:
            target, source, core_row, chip_row = second + d - depth, across.at[d - depth], from_core[d, 0], from_chip[d, 0]
        else:
            target, source, core_row, chip_row = beyond, outer.at[0], outer_core[0, 0], outer_chip[0, 0]
        lines[target, 0] = jnp.where(even_core, chip_row, core_row)
        for r in range(rows):
            lines[target, r + 1] = source[r]
        lines[target, rows + 1] = jnp.where(even_core, core_row, chip_row)
    lines[empty] = jnp.zeros(lines.shape[1:], lines.dtype)


def convolve(lines, base, depth, groups):
    rows, cols, channels = lines.shape[1] - 2, *lines.shape[2:]
    voxels = depth * rows * cols
    total = None
    for taps, arrays in groups:
        for tap in taps[::3]:
            a, b, start = tap // 9, tap // 3 % 3, (tap - taps[0]) * channels
            moved = lines[pl.ds(base + a, depth), b : b + rows].reshape(voxels, channels)
            stack = [
                array[:, start + e * channels : start + (e + 1) * channels] for e in range(3) for array in arrays
            ]
            term = lax.dot_general(
                moved, jnp.concatenate(stack, axis=0), (((1,), (1,)), ((), ())), preferred_element_type=jnp.float32
            )
            total = term if total is None else total + term
    width = total.shape[1] // 3
    col = lax.rem(lax.broadcasted_iota(jnp.int32, (voxels, width), 0), cols)
    before = jnp.where(col == 0, 0.0, pltpu.roll(total[:, :width], 1, 0))
    after = jnp.where(col == cols - 1, 0.0, pltpu.roll(total[:, 2 * width :], voxels - 1, 0))
    return before + total[:, width : 2 * width] + after


def ordered(sums):
    half = sums.shape[1] // 2
    swapped = jnp.concatenate([sums[:, half:], sums[:, :half]], axis=1)
    return jnp.where(core_parity() == 0, sums, swapped)


def pair_depth(lines):
    return (lines.shape[0] - 2) // 2


def arranged(near, far):
    far = ordered(far)
    return jnp.where(slab_x() == 0, jnp.concatenate([near, far], axis=1), jnp.concatenate([far, near], axis=1))


def back_early(lines, kernel_rows, here, there, near, far):
    depth, early = pair_depth(lines), here.shape[1] // lines.shape[3]
    base = depth * (1 - slab_x())
    near[...] = convolve(lines, base, depth, [(range(27), [kernel_rows])])
    far[...] = convolve(lines, base, depth, [(range(early), [here, there])])


def back(lines, near, far, here, there, out):
    depth, late = pair_depth(lines), here.shape[1] // lines.shape[3]
    rest = convolve(lines, depth * (1 - slab_x()), depth, [(range(27 - late, 27), [here, there])])
    out[...] = arranged(near[...], far[...] + rest).astype(out.dtype)


def kept(lines, kernel_rows, here_first, there_first, here_second, there_second, out):
    depth, early = pair_depth(lines), here_first.shape[1] // lines.shape[3]
    base, width = depth * slab_x(), kernel_rows.shape[0]
    near = convolve(lines, base, depth, [(range(27), [kernel_rows])])
    groups = [(range(early), [here_first, there_first]), (range(early, 27), [here_second, there_second])]
    out[...] = arranged(near, convolve(lines, base, depth, groups)).astype(out.dtype)


def join(kept_sums, returned, out):
    voxels, width = kept_sums.shape
    mine, theirs = kept_sums[...].astype(jnp.float32), returned[...].astype(jnp.float32)
    here = lax.div(lax.broadcasted_iota(jnp.int32, (voxels, width), 1), width // 2) == slab_x()
    near, far = jnp.where(here, mine, theirs), jnp.where(here, theirs, mine)
    near_at = pl.multiple_of(slab_y() * width, width)
    far_at = pl.multiple_of((1 - slab_y()) * width, width)
    out[:, pl.ds(near_at, width)] = near.astype(out.dtype)
    out[:, pl.ds(far_at, width)] = pltpu.roll(far, width // 2, 1).astype(out.dtype)


def four_slabs(volume, weights):
    chans = lax.axis_size("chan")
    depth, rows, cols, channels = volume.shape
    voxels = depth * rows * cols
    kernel_rows = weights.T
    width, depth_of_sum = kernel_rows.shape

    def send(array, target):
        every = [(s * chans + c, target(s, c)) for s in range(4) for c in range(chans)]
        pairs = [(source, s * chans + c) for source, (s, c) in every if 0 <= s < 4 and 0 <= c < chans]
        return lax.ppermute(array, BOTH, pairs)

    def across_x(s, c):
        return s ^ 1, c

    def across_y(s, c):
        return s ^ 2, c

    def other_core(s, c):
        return s, c ^ 1

    def next_chip(s, c):
        return s, c + (1 if c % 2 else -1)

    across = send(volume, across_x)
    early = EARLY_TAPS * channels
    pieces = [like((width // 2, early), weights), like((width // 2, depth_of_sum - early), weights)]
    first, second, block = call(
        fetch,
        [pltpu.with_memory_space_constraint(x, pltpu.HBM) for x in (volume, kernel_rows)],
        [*pieces, like(volume.shape, volume)],
        places=[pl.BlockSpec(memory_space=pltpu.HBM)] * 2,
        scratch=[pltpu.SemaphoreType.DMA((3,))],
    )
    here_first = send(first, across_y)
    second, across = lax.optimization_barrier((second, across))
    (plane,) = call(border, (block, across), [like((1, rows, cols, channels), volume)], BORDER_COST)
    outer = send(plane, across_y)
    here_second = send(second, across_y)
    edge, outer_edge = like((2 * depth, 1, cols, channels), volume), like((1, 1, cols, channels), volume)
    to_core, to_chip = call(edges, (block, across), [edge, edge], EDGES_COST)
    from_core, from_chip = send(to_core, other_core), send(to_chip, next_chip)
    outer, here_first = lax.optimization_barrier((outer, here_first))
    to_core, to_chip = call(outer_edges, (outer,), [outer_edge, outer_edge], OUTER_EDGES_COST)
    outer_core, outer_chip = send(to_core, other_core), send(to_chip, next_chip)
    here_first, outer_core = lax.optimization_barrier((here_first, outer_core))
    there_first = send(here_first, other_core)
    here_second, outer_core = lax.optimization_barrier((here_second, outer_core))
    there_second = send(here_second, other_core)
    (lines,) = call(
        extend,
        (block, across, outer, from_core, from_chip, outer_core, outer_chip),
        [like((2 * depth + 2, rows + 2, cols, channels), volume)],
        EXTEND_COST,
    )
    work = 2 * voxels * depth_of_sum * width
    both, sums = like((voxels, 2 * width), volume), jax.ShapeDtypeStruct((voxels, width), jnp.float32)
    near, far = call(back_early, (lines, kernel_rows, here_first, there_first), [sums, sums], work)
    (sent,) = call(back, (lines, near, far, here_second, there_second), [both], work)
    returned = send(sent, across_x)
    (mine,) = call(
        kept, (lines, kernel_rows, here_first, there_first, here_second, there_second), [both], 2 * work
    )
    (out,) = call(join, (mine, returned), [like((voxels, 4 * width), volume)])
    return out.reshape(volume.shape)


def halo(block, axis, dim):
    count = lax.axis_size(axis)
    forward = [(i, i + 1) for i in range(count - 1)]
    backward = [(target, source) for source, target in forward]
    extent = block.shape[dim]
    low = lax.ppermute(lax.slice_in_dim(block, extent - 1, extent, axis=dim), axis, forward)
    high = lax.ppermute(lax.slice_in_dim(block, 0, 1, axis=dim), axis, backward)
    return jnp.concatenate([low, block, high], axis=dim)


def whole(lines, kernel_rows, out):
    out[...] = convolve(lines, 0, lines.shape[0] - 2, [(range(27), [kernel_rows])]).astype(out.dtype)


def any_slabs(volume, weights):
    gathered = lax.all_gather(weights.T, "slab", axis=0, tiled=True)
    lines = halo(halo(volume, "slab", 0), "chan", 1)
    voxels, (width, depth_of_sum) = volume.size // volume.shape[-1], gathered.shape
    (out,) = call(whole, (lines, gathered), [like((voxels, width), volume)], 2 * voxels * depth_of_sum * width)
    return out.reshape(volume.shape)


def local(volume, weights):
    if lax.axis_size("slab") == 4 and lax.axis_size("chan") % 2 == 0:
        return four_slabs(volume, weights)
    return any_slabs(volume, weights)


def solution(mesh):
    placed = (P("slab", "chan", None, None), P(None, "slab"))
    return jax.shard_map(
        local, mesh=mesh, in_specs=placed, out_specs=P("slab", "chan", None, None), check_vma=False
    )
```

```python
import jax
import jax.numpy as jnp
from jax import lax
from jax.experimental import pallas as pl
from jax.experimental.pallas import tpu as pltpu
from jax.sharding import PartitionSpec as P

BOTH = ("slab", "chan")
VMEM_LIMIT = 24 * 1024 * 1024
EARLY_TAPS = 9
BORDER_COST, EDGES_COST, OUTER_EDGE_COST, EXTEND_COST = 10**9, 0, 3 * 10**9, 3 * 10**9


def call(kernel, operands, outs, flops=0, places=None, scratch=()):
    size = sum(x.size * x.dtype.itemsize for x in (*operands, *outs))
    vmem = pl.BlockSpec(memory_space=pltpu.VMEM)
    return pl.pallas_call(
        kernel,
        out_shape=outs,
        in_specs=places or [vmem] * len(operands),
        out_specs=[vmem] * len(outs),
        scratch_shapes=scratch,
        compiler_params=pltpu.CompilerParams(vmem_limit_bytes=VMEM_LIMIT),
        cost_estimate=pl.CostEstimate(flops=flops, bytes_accessed=size, transcendentals=0),
        name=kernel.__name__,
    )(*operands)


def like(shape, array):
    return jax.ShapeDtypeStruct(shape, array.dtype)


def core_parity():
    return lax.rem(lax.axis_index("chan"), 2)


def slab_x():
    return lax.rem(lax.axis_index("slab"), 2)


def slab_y():
    return lax.div(lax.axis_index("slab"), 2)


def half_rows(kernel_rows, piece, start):
    count = piece.shape[0]
    rows = pl.ds(pl.multiple_of(core_parity() * count, count), count)
    return kernel_rows.at[rows, pl.ds(start, piece.shape[1])]


def fetch(kernel_rows, first, sem):
    copy = pltpu.make_async_copy(half_rows(kernel_rows, first, 0), first, sem)
    copy.start()
    copy.wait()


def fetch_rest(volume, kernel_rows, first, second, block, sems):
    copies = [
        pltpu.make_async_copy(half_rows(kernel_rows, second, first.shape[1]), second, sems.at[0]),
        pltpu.make_async_copy(volume, block, sems.at[1]),
    ]
    for copy in copies:
        copy.start()
    for copy in copies:
        copy.wait()


def border(block, across, out):
    plane = (block.shape[0] - 1) * (1 - slab_y())
    for r in range(block.shape[1]):
        out[0, r] = jnp.where(slab_x() == slab_y(), across[plane, r], block[plane, r])


def edges(block, across, to_core, to_chip):
    depth, rows = block.shape[:2]
    core = core_parity()
    for out, row in ((to_core, (rows - 1) * (1 - core)), (to_chip, (rows - 1) * core)):
        for d in range(depth):
            out[d, 0] = block[d, row]
            out[depth + d, 0] = across[d, row]


def outer_edge(outer, to_core):
    to_core[0, 0] = outer[0, (outer.shape[1] - 1) * (1 - core_parity())]


def extend(block, across, outer, from_core, from_chip, outer_core, outer_chip, lines):
    depth, rows = block.shape[:2]
    even_core = core_parity() == 0
    first, second = depth * slab_x() + 1, depth * (1 - slab_x()) + 1
    beyond = (2 * depth + 1) * (1 - slab_y())
    empty = (2 * depth + 1) * slab_y()
    for d in range(2 * depth + 1):
        if d < depth:
            target, source, core_row, chip_row = first + d, block.at[d], from_core[d, 0], from_chip[d, 0]
        elif d < 2 * depth:
            target, source, core_row, chip_row = second + d - depth, across.at[d - depth], from_core[d, 0], from_chip[d, 0]
        else:
            target, source = beyond, outer.at[0]
            core_row, chip_row = outer_core[0, 0], outer_chip[0, (rows - 1) * (1 - core_parity())]
        lines[target, 0] = jnp.where(even_core, chip_row, core_row)
        for r in range(rows):
            lines[target, r + 1] = source[r]
        lines[target, rows + 1] = jnp.where(even_core, core_row, chip_row)
    lines[empty] = jnp.zeros(lines.shape[1:], lines.dtype)


def convolve(lines, base, depth, groups):
    rows, cols, channels = lines.shape[1] - 2, *lines.shape[2:]
    voxels = depth * rows * cols
    total = None
    for taps, arrays in groups:
        for tap in taps[::3]:
            a, b, start = tap // 9, tap // 3 % 3, (tap - taps[0]) * channels
            moved = lines[pl.ds(base + a, depth), b : b + rows].reshape(voxels, channels)
            stack = [
                array[:, start + e * channels : start + (e + 1) * channels] for e in range(3) for array in arrays
            ]
            term = lax.dot_general(
                moved, jnp.concatenate(stack, axis=0), (((1,), (1,)), ((), ())), preferred_element_type=jnp.float32
            )
            total = term if total is None else total + term
    width = total.shape[1] // 3
    col = lax.rem(lax.broadcasted_iota(jnp.int32, (voxels, width), 0), cols)
    before = jnp.where(col == 0, 0.0, pltpu.roll(total[:, :width], 1, 0))
    after = jnp.where(col == cols - 1, 0.0, pltpu.roll(total[:, 2 * width :], voxels - 1, 0))
    return before + total[:, width : 2 * width] + after


def ordered(sums):
    half = sums.shape[1] // 2
    swapped = jnp.concatenate([sums[:, half:], sums[:, :half]], axis=1)
    return jnp.where(core_parity() == 0, sums, swapped)


def pair_depth(lines):
    return (lines.shape[0] - 2) // 2


def arranged(near, far):
    far = ordered(far)
    return jnp.where(slab_x() == 0, jnp.concatenate([near, far], axis=1), jnp.concatenate([far, near], axis=1))


def back_early(lines, kernel_rows, here, there, near, far):
    depth, early = pair_depth(lines), here.shape[1] // lines.shape[3]
    base = depth * (1 - slab_x())
    near[...] = convolve(lines, base, depth, [(range(27), [kernel_rows])])
    far[...] = convolve(lines, base, depth, [(range(early), [here, there])])


def back(lines, near, far, here, there, out):
    depth, late = pair_depth(lines), here.shape[1] // lines.shape[3]
    rest = convolve(lines, depth * (1 - slab_x()), depth, [(range(27 - late, 27), [here, there])])
    out[...] = arranged(near[...], far[...] + rest).astype(out.dtype)


def kept(lines, kernel_rows, here_first, there_first, here_second, there_second, out):
    depth, early = pair_depth(lines), here_first.shape[1] // lines.shape[3]
    base, width = depth * slab_x(), kernel_rows.shape[0]
    near = convolve(lines, base, depth, [(range(27), [kernel_rows])])
    groups = [(range(early), [here_first, there_first]), (range(early, 27), [here_second, there_second])]
    out[...] = arranged(near, convolve(lines, base, depth, groups)).astype(out.dtype)


def join(kept_sums, returned, out):
    voxels, width = kept_sums.shape
    mine, theirs = kept_sums[...].astype(jnp.float32), returned[...].astype(jnp.float32)
    here = lax.div(lax.broadcasted_iota(jnp.int32, (voxels, width), 1), width // 2) == slab_x()
    near, far = jnp.where(here, mine, theirs), jnp.where(here, theirs, mine)
    near_at = pl.multiple_of(slab_y() * width, width)
    far_at = pl.multiple_of((1 - slab_y()) * width, width)
    out[:, pl.ds(near_at, width)] = near.astype(out.dtype)
    out[:, pl.ds(far_at, width)] = pltpu.roll(far, width // 2, 1).astype(out.dtype)


def four_slabs(volume, weights):
    chans = lax.axis_size("chan")
    depth, rows, cols, channels = volume.shape
    voxels = depth * rows * cols
    kernel_rows = weights.T
    width, depth_of_sum = kernel_rows.shape

    def send(array, target):
        every = [(s * chans + c, target(s, c)) for s in range(4) for c in range(chans)]
        pairs = [(source, s * chans + c) for source, (s, c) in every if 0 <= s < 4 and 0 <= c < chans]
        return lax.ppermute(array, BOTH, pairs)

    def across_x(s, c):
        return s ^ 1, c

    def across_y(s, c):
        return s ^ 2, c

    def other_core(s, c):
        return s, c ^ 1

    def next_chip(s, c):
        return s, c + (1 if c % 2 else -1)

    across = send(volume, across_x)
    early = EARLY_TAPS * channels
    pieces = [like((width // 2, early), weights), like((width // 2, depth_of_sum - early), weights)]
    hbm = pl.BlockSpec(memory_space=pltpu.HBM)
    block_in_hbm, rows_in_hbm = [pltpu.with_memory_space_constraint(x, pltpu.HBM) for x in (volume, kernel_rows)]
    (first,) = call(fetch, (rows_in_hbm,), pieces[:1], places=[hbm], scratch=[pltpu.SemaphoreType.DMA])
    here_first = send(first, across_y)
    second, block = call(
        fetch_rest,
        (block_in_hbm, rows_in_hbm, first),
        [pieces[1], like(volume.shape, volume)],
        0,
        places=[hbm, hbm, pl.BlockSpec(memory_space=pl.ANY)],
        scratch=[pltpu.SemaphoreType.DMA((2,))],
    )
    second, across = lax.optimization_barrier((second, across))
    (plane,) = call(border, (block, across), [like((1, rows, cols, channels), volume)], BORDER_COST)
    outer = send(plane, across_y)
    here_second = send(second, across_y)
    edge, line = like((2 * depth, 1, cols, channels), volume), like((1, 1, cols, channels), volume)
    to_core, to_chip = call(edges, (block, across), [edge, edge], EDGES_COST)
    from_core, from_chip = send(to_core, other_core), send(to_chip, next_chip)
    outer, here_first = lax.optimization_barrier((outer, here_first))
    outer_chip = send(outer, next_chip)
    (to_core,) = call(outer_edge, (outer,), [line], OUTER_EDGE_COST)
    outer_core = send(to_core, other_core)
    here_first, outer_core = lax.optimization_barrier((here_first, outer_core))
    there_first = send(here_first, other_core)
    here_second, outer_core = lax.optimization_barrier((here_second, outer_core))
    there_second = send(here_second, other_core)
    (lines,) = call(
        extend,
        (block, across, outer, from_core, from_chip, outer_core, outer_chip),
        [like((2 * depth + 2, rows + 2, cols, channels), volume)],
        EXTEND_COST,
    )
    work = 2 * voxels * depth_of_sum * width
    both, sums = like((voxels, 2 * width), volume), jax.ShapeDtypeStruct((voxels, width), jnp.float32)
    near, far = call(back_early, (lines, kernel_rows, here_first, there_first), [sums, sums], work)
    (sent,) = call(back, (lines, near, far, here_second, there_second), [both], work)
    returned = send(sent, across_x)
    (mine,) = call(
        kept, (lines, kernel_rows, here_first, there_first, here_second, there_second), [both], 2 * work
    )
    (out,) = call(join, (mine, returned), [like((voxels, 4 * width), volume)])
    return out.reshape(volume.shape)


def halo(block, axis, dim):
    count = lax.axis_size(axis)
    forward = [(i, i + 1) for i in range(count - 1)]
    backward = [(target, source) for source, target in forward]
    extent = block.shape[dim]
    low = lax.ppermute(lax.slice_in_dim(block, extent - 1, extent, axis=dim), axis, forward)
    high = lax.ppermute(lax.slice_in_dim(block, 0, 1, axis=dim), axis, backward)
    return jnp.concatenate([low, block, high], axis=dim)


def whole(lines, kernel_rows, out):
    out[...] = convolve(lines, 0, lines.shape[0] - 2, [(range(27), [kernel_rows])]).astype(out.dtype)


def any_slabs(volume, weights):
    gathered = lax.all_gather(weights.T, "slab", axis=0, tiled=True)
    lines = halo(halo(volume, "slab", 0), "chan", 1)
    voxels, (width, depth_of_sum) = volume.size // volume.shape[-1], gathered.shape
    (out,) = call(whole, (lines, gathered), [like((voxels, width), volume)], 2 * voxels * depth_of_sum * width)
    return out.reshape(volume.shape)


def local(volume, weights):
    if lax.axis_size("slab") == 4 and lax.axis_size("chan") % 2 == 0:
        return four_slabs(volume, weights)
    return any_slabs(volume, weights)


def solution(mesh):
    placed = (P("slab", "chan", None, None), P(None, "slab"))
    return jax.shard_map(
        local, mesh=mesh, in_specs=placed, out_specs=P("slab", "chan", None, None), check_vma=False
    )
```

```python
import jax
import jax.numpy as jnp
from jax import lax
from jax.experimental import pallas as pl
from jax.experimental.pallas import tpu as pltpu
from jax.sharding import PartitionSpec as P

BOTH = ("slab", "chan")
VMEM_LIMIT = 24 * 1024 * 1024
EARLY_TAPS = 9
BORDER_COST, EDGES_COST, OUTER_EDGES_COST, EXTEND_COST = 1 * 10**9, 5 * 10**9, 8 * 10**9, 3 * 10**9


def call(kernel, operands, outs, flops=0, places=None, scratch=()):
    size = sum(x.size * x.dtype.itemsize for x in (*operands, *outs))
    vmem = pl.BlockSpec(memory_space=pltpu.VMEM)
    return pl.pallas_call(
        kernel,
        out_shape=outs,
        in_specs=places or [vmem] * len(operands),
        out_specs=[vmem] * len(outs),
        scratch_shapes=scratch,
        compiler_params=pltpu.CompilerParams(vmem_limit_bytes=VMEM_LIMIT),
        cost_estimate=pl.CostEstimate(flops=flops, bytes_accessed=size, transcendentals=0),
        name=kernel.__name__,
    )(*operands)


def like(shape, array):
    return jax.ShapeDtypeStruct(shape, array.dtype)


def core_parity():
    return lax.rem(lax.axis_index("chan"), 2)


def slab_x():
    return lax.rem(lax.axis_index("slab"), 2)


def slab_y():
    return lax.div(lax.axis_index("slab"), 2)


def half_rows(kernel_rows, piece, start):
    count = piece.shape[0]
    rows = pl.ds(pl.multiple_of(core_parity() * count, count), count)
    return kernel_rows.at[rows, pl.ds(start, piece.shape[1])]


def fetch(kernel_rows, first, sem):
    copy = pltpu.make_async_copy(half_rows(kernel_rows, first, 0), first, sem)
    copy.start()
    copy.wait()


def fetch_rest(volume, kernel_rows, first, second, block, sems):
    copies = [
        pltpu.make_async_copy(half_rows(kernel_rows, second, first.shape[1]), second, sems.at[0]),
        pltpu.make_async_copy(volume, block, sems.at[1]),
    ]
    for copy in copies:
        copy.start()
    for copy in copies:
        copy.wait()


def border(block, across, out):
    plane = (block.shape[0] - 1) * (1 - slab_y())
    for r in range(block.shape[1]):
        out[0, r] = jnp.where(slab_x() == slab_y(), across[plane, r], block[plane, r])


def edges(block, across, to_core, to_chip):
    depth, rows = block.shape[:2]
    core = core_parity()
    for out, row in ((to_core, (rows - 1) * (1 - core)), (to_chip, (rows - 1) * core)):
        for d in range(depth):
            out[d, 0] = block[d, row]
            out[depth + d, 0] = across[d, row]


def outer_edges(outer, to_core, to_chip):
    rows = outer.shape[1]
    core = core_parity()
    for out, row in ((to_core, (rows - 1) * (1 - core)), (to_chip, (rows - 1) * core)):
        out[0, 0] = outer[0, row]


def extend(block, across, outer, from_core, from_chip, outer_core, outer_chip, lines):
    depth, rows = block.shape[:2]
    even_core = core_parity() == 0
    first, second = depth * slab_x() + 1, depth * (1 - slab_x()) + 1
    beyond = (2 * depth + 1) * (1 - slab_y())
    empty = (2 * depth + 1) * slab_y()
    for d in range(2 * depth + 1):
        if d < depth:
            target, source, core_row, chip_row = first + d, block.at[d], from_core[d, 0], from_chip[d, 0]
        elif d < 2 * depth:
            target, source, core_row, chip_row = second + d - depth, across.at[d - depth], from_core[d, 0], from_chip[d, 0]
        else:
            target, source, core_row, chip_row = beyond, outer.at[0], outer_core[0, 0], outer_chip[0, 0]
        lines[target, 0] = jnp.where(even_core, chip_row, core_row)
        for r in range(rows):
            lines[target, r + 1] = source[r]
        lines[target, rows + 1] = jnp.where(even_core, core_row, chip_row)
    lines[empty] = jnp.zeros(lines.shape[1:], lines.dtype)


def convolve(lines, base, depth, groups):
    rows, cols, channels = lines.shape[1] - 2, *lines.shape[2:]
    voxels = depth * rows * cols
    total = None
    for taps, arrays in groups:
        for tap in taps[::3]:
            a, b, start = tap // 9, tap // 3 % 3, (tap - taps[0]) * channels
            moved = lines[pl.ds(base + a, depth), b : b + rows].reshape(voxels, channels)
            stack = [
                array[:, start + e * channels : start + (e + 1) * channels] for e in range(3) for array in arrays
            ]
            term = lax.dot_general(
                moved, jnp.concatenate(stack, axis=0), (((1,), (1,)), ((), ())), preferred_element_type=jnp.float32
            )
            total = term if total is None else total + term
    width = total.shape[1] // 3
    col = lax.rem(lax.broadcasted_iota(jnp.int32, (voxels, width), 0), cols)
    before = jnp.where(col == 0, 0.0, pltpu.roll(total[:, :width], 1, 0))
    after = jnp.where(col == cols - 1, 0.0, pltpu.roll(total[:, 2 * width :], voxels - 1, 0))
    return before + total[:, width : 2 * width] + after


def ordered(sums):
    half = sums.shape[1] // 2
    swapped = jnp.concatenate([sums[:, half:], sums[:, :half]], axis=1)
    return jnp.where(core_parity() == 0, sums, swapped)


def pair_depth(lines):
    return (lines.shape[0] - 2) // 2


def arranged(near, far):
    far = ordered(far)
    return jnp.where(slab_x() == 0, jnp.concatenate([near, far], axis=1), jnp.concatenate([far, near], axis=1))


def back_early(lines, kernel_rows, here, there, near, far):
    depth, early = pair_depth(lines), here.shape[1] // lines.shape[3]
    base = depth * (1 - slab_x())
    near[...] = convolve(lines, base, depth, [(range(27), [kernel_rows])])
    far[...] = convolve(lines, base, depth, [(range(early), [here, there])])


def back(lines, near, far, here, there, out):
    depth, late = pair_depth(lines), here.shape[1] // lines.shape[3]
    rest = convolve(lines, depth * (1 - slab_x()), depth, [(range(27 - late, 27), [here, there])])
    out[...] = arranged(near[...], far[...] + rest).astype(out.dtype)


def kept(lines, kernel_rows, here_first, there_first, here_second, there_second, out):
    depth, early = pair_depth(lines), here_first.shape[1] // lines.shape[3]
    base, width = depth * slab_x(), kernel_rows.shape[0]
    near = convolve(lines, base, depth, [(range(27), [kernel_rows])])
    groups = [(range(early), [here_first, there_first]), (range(early, 27), [here_second, there_second])]
    out[...] = arranged(near, convolve(lines, base, depth, groups)).astype(out.dtype)


def join(kept_sums, returned, out):
    voxels, width = kept_sums.shape
    mine, theirs = kept_sums[...].astype(jnp.float32), returned[...].astype(jnp.float32)
    here = lax.div(lax.broadcasted_iota(jnp.int32, (voxels, width), 1), width // 2) == slab_x()
    near, far = jnp.where(here, mine, theirs), jnp.where(here, theirs, mine)
    near_at = pl.multiple_of(slab_y() * width, width)
    far_at = pl.multiple_of((1 - slab_y()) * width, width)
    out[:, pl.ds(near_at, width)] = near.astype(out.dtype)
    out[:, pl.ds(far_at, width)] = pltpu.roll(far, width // 2, 1).astype(out.dtype)


def four_slabs(volume, weights):
    chans = lax.axis_size("chan")
    depth, rows, cols, channels = volume.shape
    voxels = depth * rows * cols
    kernel_rows = weights.T
    width, depth_of_sum = kernel_rows.shape

    def send(array, target):
        every = [(s * chans + c, target(s, c)) for s in range(4) for c in range(chans)]
        pairs = [(source, s * chans + c) for source, (s, c) in every if 0 <= s < 4 and 0 <= c < chans]
        return lax.ppermute(array, BOTH, pairs)

    def across_x(s, c):
        return s ^ 1, c

    def across_y(s, c):
        return s ^ 2, c

    def other_core(s, c):
        return s, c ^ 1

    def next_chip(s, c):
        return s, c + (1 if c % 2 else -1)

    across = send(volume, across_x)
    early = EARLY_TAPS * channels
    pieces = [like((width // 2, early), weights), like((width // 2, depth_of_sum - early), weights)]
    hbm = pl.BlockSpec(memory_space=pltpu.HBM)
    block_in_hbm, rows_in_hbm = [pltpu.with_memory_space_constraint(x, pltpu.HBM) for x in (volume, kernel_rows)]
    (first,) = call(fetch, (rows_in_hbm,), pieces[:1], places=[hbm], scratch=[pltpu.SemaphoreType.DMA])
    here_first = send(first, across_y)
    second, block = call(
        fetch_rest,
        (block_in_hbm, rows_in_hbm, first),
        [pieces[1], like(volume.shape, volume)],
        0,
        places=[hbm, hbm, pl.BlockSpec(memory_space=pl.ANY)],
        scratch=[pltpu.SemaphoreType.DMA((2,))],
    )
    second, across = lax.optimization_barrier((second, across))
    (plane,) = call(border, (block, across), [like((1, rows, cols, channels), volume)], BORDER_COST)
    outer = send(plane, across_y)
    here_second = send(second, across_y)
    edge, outer_edge = like((2 * depth, 1, cols, channels), volume), like((1, 1, cols, channels), volume)
    to_core, to_chip = call(edges, (block, across), [edge, edge], EDGES_COST)
    from_core, from_chip = send(to_core, other_core), send(to_chip, next_chip)
    outer, here_first = lax.optimization_barrier((outer, here_first))
    to_core, to_chip = call(outer_edges, (outer,), [outer_edge, outer_edge], OUTER_EDGES_COST)
    outer_core, outer_chip = send(to_core, other_core), send(to_chip, next_chip)
    here_first, outer_core = lax.optimization_barrier((here_first, outer_core))
    there_first = send(here_first, other_core)
    here_second, outer_core = lax.optimization_barrier((here_second, outer_core))
    there_second = send(here_second, other_core)
    (lines,) = call(
        extend,
        (block, across, outer, from_core, from_chip, outer_core, outer_chip),
        [like((2 * depth + 2, rows + 2, cols, channels), volume)],
        EXTEND_COST,
    )
    work = 2 * voxels * depth_of_sum * width
    both, sums = like((voxels, 2 * width), volume), jax.ShapeDtypeStruct((voxels, width), jnp.float32)
    near, far = call(back_early, (lines, kernel_rows, here_first, there_first), [sums, sums], work)
    (sent,) = call(back, (lines, near, far, here_second, there_second), [both], work)
    returned = send(sent, across_x)
    (mine,) = call(
        kept, (lines, kernel_rows, here_first, there_first, here_second, there_second), [both], 2 * work
    )
    (out,) = call(join, (mine, returned), [like((voxels, 4 * width), volume)])
    return out.reshape(volume.shape)


def halo(block, axis, dim):
    count = lax.axis_size(axis)
    forward = [(i, i + 1) for i in range(count - 1)]
    backward = [(target, source) for source, target in forward]
    extent = block.shape[dim]
    low = lax.ppermute(lax.slice_in_dim(block, extent - 1, extent, axis=dim), axis, forward)
    high = lax.ppermute(lax.slice_in_dim(block, 0, 1, axis=dim), axis, backward)
    return jnp.concatenate([low, block, high], axis=dim)


def whole(lines, kernel_rows, out):
    out[...] = convolve(lines, 0, lines.shape[0] - 2, [(range(27), [kernel_rows])]).astype(out.dtype)


def any_slabs(volume, weights):
    gathered = lax.all_gather(weights.T, "slab", axis=0, tiled=True)
    lines = halo(halo(volume, "slab", 0), "chan", 1)
    voxels, (width, depth_of_sum) = volume.size // volume.shape[-1], gathered.shape
    (out,) = call(whole, (lines, gathered), [like((voxels, width), volume)], 2 * voxels * depth_of_sum * width)
    return out.reshape(volume.shape)


def local(volume, weights):
    if lax.axis_size("slab") == 4 and lax.axis_size("chan") % 2 == 0:
        return four_slabs(volume, weights)
    return any_slabs(volume, weights)


def solution(mesh):
    placed = (P("slab", "chan", None, None), P(None, "slab"))
    return jax.shard_map(
        local, mesh=mesh, in_specs=placed, out_specs=P("slab", "chan", None, None), check_vma=False
    )
```

```python
import jax
import jax.numpy as jnp
from jax import lax
from jax.experimental import pallas as pl
from jax.experimental.pallas import tpu as pltpu
from jax.sharding import PartitionSpec as P

BOTH = ("slab", "chan")
VMEM_LIMIT = 24 * 1024 * 1024
EARLY_TAPS = 9
BORDER_COST, EDGES_COST, OUTER_EDGES_COST, EXTEND_COST = 1 * 10**9, 5 * 10**9, 8 * 10**9, 3 * 10**9


def call(kernel, operands, outs, flops=0, places=None, out_place=None, scratch=()):
    size = sum(x.size * x.dtype.itemsize for x in (*operands, *outs))
    vmem = pl.BlockSpec(memory_space=pltpu.VMEM)
    return pl.pallas_call(
        kernel,
        out_shape=outs,
        in_specs=places or [vmem] * len(operands),
        out_specs=[out_place or vmem] * len(outs),
        scratch_shapes=scratch,
        compiler_params=pltpu.CompilerParams(vmem_limit_bytes=VMEM_LIMIT),
        cost_estimate=pl.CostEstimate(flops=flops, bytes_accessed=size, transcendentals=0),
        name=kernel.__name__,
    )(*operands)


def like(shape, array):
    return jax.ShapeDtypeStruct(shape, array.dtype)


def core_parity():
    return lax.rem(lax.axis_index("chan"), 2)


def slab_x():
    return lax.rem(lax.axis_index("slab"), 2)


def slab_y():
    return lax.div(lax.axis_index("slab"), 2)


def half_rows(kernel_rows, piece, start):
    count = piece.shape[0]
    rows = pl.ds(pl.multiple_of(core_parity() * count, count), count)
    return kernel_rows.at[rows, pl.ds(start, piece.shape[1])]


def fetch(kernel_rows, first, sem):
    copy = pltpu.make_async_copy(half_rows(kernel_rows, first, 0), first, sem)
    copy.start()
    copy.wait()


def fetch_rest(volume, kernel_rows, first, second, block, sems):
    copies = [
        pltpu.make_async_copy(half_rows(kernel_rows, second, first.shape[1]), second, sems.at[0]),
        pltpu.make_async_copy(volume, block, sems.at[1]),
    ]
    for copy in copies:
        copy.start()
    for copy in copies:
        copy.wait()


def border(block, across, out):
    plane = (block.shape[0] - 1) * (1 - slab_y())
    for r in range(block.shape[1]):
        out[0, r] = jnp.where(slab_x() == slab_y(), across[plane, r], block[plane, r])


def edges(block, across, to_core, to_chip):
    depth, rows = block.shape[:2]
    core = core_parity()
    for out, row in ((to_core, (rows - 1) * (1 - core)), (to_chip, (rows - 1) * core)):
        for d in range(depth):
            out[d, 0] = block[d, row]
            out[depth + d, 0] = across[d, row]


def outer_edges(outer, to_core, to_chip):
    rows = outer.shape[1]
    core = core_parity()
    for out, row in ((to_core, (rows - 1) * (1 - core)), (to_chip, (rows - 1) * core)):
        out[0, 0] = outer[0, row]


def extend(block, across, outer, from_core, from_chip, outer_core, outer_chip, lines):
    depth, rows = block.shape[:2]
    even_core = core_parity() == 0
    first, second = depth * slab_x() + 1, depth * (1 - slab_x()) + 1
    beyond = (2 * depth + 1) * (1 - slab_y())
    empty = (2 * depth + 1) * slab_y()
    for d in range(2 * depth + 1):
        if d < depth:
            target, source, core_row, chip_row = first + d, block.at[d], from_core[d, 0], from_chip[d, 0]
        elif d < 2 * depth:
            target, source, core_row, chip_row = second + d - depth, across.at[d - depth], from_core[d, 0], from_chip[d, 0]
        else:
            target, source, core_row, chip_row = beyond, outer.at[0], outer_core[0, 0], outer_chip[0, 0]
        lines[target, 0] = jnp.where(even_core, chip_row, core_row)
        for r in range(rows):
            lines[target, r + 1] = source[r]
        lines[target, rows + 1] = jnp.where(even_core, core_row, chip_row)
    lines[empty] = jnp.zeros(lines.shape[1:], lines.dtype)


def convolve(lines, base, depth, groups):
    rows, cols, channels = lines.shape[1] - 2, *lines.shape[2:]
    voxels = depth * rows * cols
    total = None
    for taps, arrays in groups:
        for tap in taps[::3]:
            a, b, start = tap // 9, tap // 3 % 3, (tap - taps[0]) * channels
            moved = lines[pl.ds(base + a, depth), b : b + rows].reshape(voxels, channels)
            stack = [
                array[:, start + e * channels : start + (e + 1) * channels] for e in range(3) for array in arrays
            ]
            term = lax.dot_general(
                moved, jnp.concatenate(stack, axis=0), (((1,), (1,)), ((), ())), preferred_element_type=jnp.float32
            )
            total = term if total is None else total + term
    width = total.shape[1] // 3
    col = lax.rem(lax.broadcasted_iota(jnp.int32, (voxels, width), 0), cols)
    before = jnp.where(col == 0, 0.0, pltpu.roll(total[:, :width], 1, 0))
    after = jnp.where(col == cols - 1, 0.0, pltpu.roll(total[:, 2 * width :], voxels - 1, 0))
    return before + total[:, width : 2 * width] + after


def ordered(sums):
    half = sums.shape[1] // 2
    swapped = jnp.concatenate([sums[:, half:], sums[:, :half]], axis=1)
    return jnp.where(core_parity() == 0, sums, swapped)


def pair_depth(lines):
    return (lines.shape[0] - 2) // 2


def arranged(near, far):
    far = ordered(far)
    return jnp.where(slab_x() == 0, jnp.concatenate([near, far], axis=1), jnp.concatenate([far, near], axis=1))


def back_early(lines, kernel_rows, here, there, near, far):
    depth, early = pair_depth(lines), here.shape[1] // lines.shape[3]
    base = depth * (1 - slab_x())
    near[...] = convolve(lines, base, depth, [(range(27), [kernel_rows])])
    far[...] = convolve(lines, base, depth, [(range(early), [here, there])])


def back(lines, near, far, here, there, out):
    depth, late = pair_depth(lines), here.shape[1] // lines.shape[3]
    rest = convolve(lines, depth * (1 - slab_x()), depth, [(range(27 - late, 27), [here, there])])
    out[...] = arranged(near[...], far[...] + rest).astype(out.dtype)


def kept(lines, kernel_rows, here_first, there_first, here_second, there_second, out):
    depth, early = pair_depth(lines), here_first.shape[1] // lines.shape[3]
    base, width = depth * slab_x(), kernel_rows.shape[0]
    near = convolve(lines, base, depth, [(range(27), [kernel_rows])])
    groups = [(range(early), [here_first, there_first]), (range(early, 27), [here_second, there_second])]
    out[...] = arranged(near, convolve(lines, base, depth, groups)).astype(out.dtype)


def join(kept_sums, returned, out, tiles, sems):
    voxels, width = kept_sums.shape
    mine, theirs = kept_sums[...].astype(jnp.float32), returned[...].astype(jnp.float32)
    here = lax.div(lax.broadcasted_iota(jnp.int32, (voxels, width), 1), width // 2) == slab_x()
    near_at = pl.multiple_of(slab_y() * width, width)
    far_at = pl.multiple_of((1 - slab_y()) * width, width)
    near_copy = pltpu.make_async_copy(tiles.at[0], out.at[:, pl.ds(near_at, width)], sems.at[0])
    far_copy = pltpu.make_async_copy(tiles.at[1], out.at[:, pl.ds(far_at, width)], sems.at[1])
    tiles[0] = jnp.where(here, mine, theirs).astype(out.dtype)
    near_copy.start()
    tiles[1] = pltpu.roll(jnp.where(here, theirs, mine), width // 2, 1).astype(out.dtype)
    far_copy.start()
    near_copy.wait()
    far_copy.wait()


def four_slabs(volume, weights):
    chans = lax.axis_size("chan")
    depth, rows, cols, channels = volume.shape
    voxels = depth * rows * cols
    kernel_rows = weights.T
    width, depth_of_sum = kernel_rows.shape

    def send(array, target):
        every = [(s * chans + c, target(s, c)) for s in range(4) for c in range(chans)]
        pairs = [(source, s * chans + c) for source, (s, c) in every if 0 <= s < 4 and 0 <= c < chans]
        return lax.ppermute(array, BOTH, pairs)

    def across_x(s, c):
        return s ^ 1, c

    def across_y(s, c):
        return s ^ 2, c

    def other_core(s, c):
        return s, c ^ 1

    def next_chip(s, c):
        return s, c + (1 if c % 2 else -1)

    across = send(volume, across_x)
    early = EARLY_TAPS * channels
    pieces = [like((width // 2, early), weights), like((width // 2, depth_of_sum - early), weights)]
    hbm = pl.BlockSpec(memory_space=pltpu.HBM)
    block_in_hbm, rows_in_hbm = [pltpu.with_memory_space_constraint(x, pltpu.HBM) for x in (volume, kernel_rows)]
    (first,) = call(fetch, (rows_in_hbm,), pieces[:1], places=[hbm], scratch=[pltpu.SemaphoreType.DMA])
    here_first = send(first, across_y)
    second, block = call(
        fetch_rest,
        (block_in_hbm, rows_in_hbm, first),
        [pieces[1], like(volume.shape, volume)],
        0,
        places=[hbm, hbm, pl.BlockSpec(memory_space=pl.ANY)],
        scratch=[pltpu.SemaphoreType.DMA((2,))],
    )
    second, across = lax.optimization_barrier((second, across))
    (plane,) = call(border, (block, across), [like((1, rows, cols, channels), volume)], BORDER_COST)
    outer = send(plane, across_y)
    here_second = send(second, across_y)
    edge, outer_edge = like((2 * depth, 1, cols, channels), volume), like((1, 1, cols, channels), volume)
    to_core, to_chip = call(edges, (block, across), [edge, edge], EDGES_COST)
    from_core, from_chip = send(to_core, other_core), send(to_chip, next_chip)
    outer, here_first = lax.optimization_barrier((outer, here_first))
    to_core, to_chip = call(outer_edges, (outer,), [outer_edge, outer_edge], OUTER_EDGES_COST)
    outer_core, outer_chip = send(to_core, other_core), send(to_chip, next_chip)
    here_first, outer_core = lax.optimization_barrier((here_first, outer_core))
    there_first = send(here_first, other_core)
    here_second, outer_core = lax.optimization_barrier((here_second, outer_core))
    there_second = send(here_second, other_core)
    (lines,) = call(
        extend,
        (block, across, outer, from_core, from_chip, outer_core, outer_chip),
        [like((2 * depth + 2, rows + 2, cols, channels), volume)],
        EXTEND_COST,
    )
    work = 2 * voxels * depth_of_sum * width
    both, sums = like((voxels, 2 * width), volume), jax.ShapeDtypeStruct((voxels, width), jnp.float32)
    near, far = call(back_early, (lines, kernel_rows, here_first, there_first), [sums, sums], work)
    (sent,) = call(back, (lines, near, far, here_second, there_second), [both], work)
    returned = send(sent, across_x)
    (mine,) = call(
        kept, (lines, kernel_rows, here_first, there_first, here_second, there_second), [both], 2 * work
    )
    (out,) = call(
        join,
        (mine, returned),
        [like((voxels, 4 * width), volume)],
        out_place=pl.BlockSpec(memory_space=pltpu.HBM),
        scratch=[pltpu.VMEM((2, voxels, 2 * width), volume.dtype), pltpu.SemaphoreType.DMA((2,))],
    )
    return out.reshape(volume.shape)


def halo(block, axis, dim):
    count = lax.axis_size(axis)
    forward = [(i, i + 1) for i in range(count - 1)]
    backward = [(target, source) for source, target in forward]
    extent = block.shape[dim]
    low = lax.ppermute(lax.slice_in_dim(block, extent - 1, extent, axis=dim), axis, forward)
    high = lax.ppermute(lax.slice_in_dim(block, 0, 1, axis=dim), axis, backward)
    return jnp.concatenate([low, block, high], axis=dim)


def whole(lines, kernel_rows, out):
    out[...] = convolve(lines, 0, lines.shape[0] - 2, [(range(27), [kernel_rows])]).astype(out.dtype)


def any_slabs(volume, weights):
    gathered = lax.all_gather(weights.T, "slab", axis=0, tiled=True)
    lines = halo(halo(volume, "slab", 0), "chan", 1)
    voxels, (width, depth_of_sum) = volume.size // volume.shape[-1], gathered.shape
    (out,) = call(whole, (lines, gathered), [like((voxels, width), volume)], 2 * voxels * depth_of_sum * width)
    return out.reshape(volume.shape)


def local(volume, weights):
    if lax.axis_size("slab") == 4 and lax.axis_size("chan") % 2 == 0:
        return four_slabs(volume, weights)
    return any_slabs(volume, weights)


def solution(mesh):
    placed = (P("slab", "chan", None, None), P(None, "slab"))
    return jax.shard_map(
        local, mesh=mesh, in_specs=placed, out_specs=P("slab", "chan", None, None), check_vma=False
    )
```
